32 devices in a mesh: row: 4 (over y, core), col: 8 (over z, x).
Axes of the slice: x: 2, y: 2, z: 4, core: 2. Of those that a mesh axis runs over, the one named last changes fastest.
Arguments:
- query_matrix: bfloat16 [32, 128, 768], P('row', 'col'), may hold values from -6 to 16.133757
- key_matrix: bfloat16 [32, 128, 768], P('row', 'col'), may hold values from -6 to 6
- value_matrix: bfloat16 [32, 128, 768], P('row', 'col'), may hold values from -6 to 6
- tissue: int32 [32, 128], replicated, may hold values 0 or 1
- dilation_levels: int32 [16], replicated, may hold values from 0 to 2
- segment_levels: int32 [16], replicated, may hold values from 0 to 2
- output_matrix: bfloat16 [768, 768], replicated, may hold values from -0.21875 to 0.21875
Outputs:
- encoded: bfloat16 [32, 128, 768], P('row', 'col')
The draws below stay inside these ranges and needn't reach their ends.
Inputs may be any that keep to these rules, and one draw needn't show every extreme that they name: 1 marks a tissue tile, 0 background. Head h uses the dilation 8 * 2^dilation_levels[h]. Head h uses segments of 128 / 2^segment_levels[h] tiles of a grid row.
All inputs are finite; a program needn't handle non-finite values.
Results may differ from the reference program's by a relative error of at most 0.0055.
Values may be sent and summed in bfloat16 or wider, within the bound.
A program may use at most 64 MiB of HBM per device.

```python
import math
import jax
import jax.numpy as jnp
import numpy as np
from jax import lax

D = 768
HEAD_COUNT = 16
DEVICE_GRID_ROWS = 8
DEVICE_GRID_COLS = 16
R = 8
DILATION_MIN = 8
GRID_ROWS = 32
GRID_COLUMNS = 128
REACHED_TILES = 16
N_ROW = 4
N_COL = 8


def draw_query_matrix(key, part):
    noise_key = jax.random.fold_in(key, 0)
    drawn = jnp.clip(jax.random.normal(noise_key, (GRID_ROWS, GRID_COLUMNS, D), jnp.float32), -6.0, 6.0)
    return drawn.astype(jnp.bfloat16)


def draw_key_matrix(key, part):
    noise_key = jax.random.fold_in(key, 7)
    drawn = jnp.clip(jax.random.normal(noise_key, (GRID_ROWS, GRID_COLUMNS, D), jnp.float32), -6.0, 6.0)
    return drawn.astype(jnp.bfloat16)


def with_ends(values, own_key, low, top_value):
    longest = values.shape.index(max(values.shape))
    spots = []
    for shift in (0, 1):
        where = [jax.random.randint(jax.random.fold_in(own_key, axis), (), 0, length) for axis, length in enumerate(values.shape)]
        where[longest] = (where[longest] + shift) % values.shape[longest]
        spots.append(tuple(where))
    return values.at[spots[0]].set(low).at[spots[1]].set(top_value)


def levels(key, shape, cuts, low, high):
    def one(axis_at, shards_of):
        draws = jax.random.uniform(jax.random.fold_in(jax.random.fold_in(key, 6), axis_at), (shards_of,), jnp.float32, low / len(cuts), high / len(cuts))
        return jnp.repeat(jnp.exp(draws), shape[axis_at] // shards_of).reshape((-1,) + (1,) * (len(shape) - axis_at - 1))

    level = one(*cuts[0])
    for cut in cuts[1:]:
        level = level * one(*cut)
    return level


def normal_values(stream_key, shape, scale, reach, cuts=(), held_as=jnp.bfloat16):
    level = levels(stream_key, shape, cuts, -0.22, 0.18) if cuts else 1.0
    drawn = jax.random.normal(stream_key, shape, jnp.float32) * scale * level
    return jnp.minimum(jnp.maximum(drawn, -reach), reach).astype(held_as)


def setup_inputs(seed: int = 0) -> dict:
    keys = jax.random.split(jax.random.key(seed), 8)
    query_matrix = draw_query_matrix(jax.random.fold_in(keys[7], 71), 0)
    key_matrix = draw_key_matrix(jax.random.fold_in(keys[7], 71), 0)
    value_matrix = normal_values(keys[2], (GRID_ROWS, GRID_COLUMNS, D), 1.0, 6.0, ((0, 4), (1, 8)))
    tissue = with_ends((jax.random.randint(keys[3], (GRID_ROWS, GRID_COLUMNS), 0, 5) < 3).astype(jnp.int32), jax.random.fold_in(keys[3], 1), 0, 1)
    dilation_levels = with_ends(jax.random.randint(keys[4], (HEAD_COUNT,), 0, 3), jax.random.fold_in(keys[4], 1), 0, 2).astype(jnp.int32)
    segment_levels = with_ends(jax.random.randint(keys[5], (HEAD_COUNT,), 0, 3), jax.random.fold_in(keys[5], 1), 0, 2).astype(jnp.int32)
    output_matrix = normal_values(keys[6], (D, D), D ** -0.5, 0.21875)
    return dict(query_matrix=query_matrix, key_matrix=key_matrix, value_matrix=value_matrix, tissue=tissue, dilation_levels=dilation_levels, segment_levels=segment_levels, output_matrix=output_matrix)


NEG_FILL = -1e+30

def window_static(device_rows, device_columns):
    region_rows = np.arange(device_rows + 2 * R) - R
    query_rows = np.arange(device_rows)
    region_cols = np.arange(device_columns + 2 * R) - R
    query_cols = np.arange(device_columns)
    near_rows = np.abs(region_rows[None, :] - query_rows[:, None]) <= R
    near_cols = np.abs(region_cols[None, :] - query_cols[:, None]) <= R
    same_rows = region_rows[None, :] == query_rows[:, None]
    same_cols = region_cols[None, :] == query_cols[:, None]
    near_both = near_rows[:, None, :, None] & near_cols[None, :, None, :]
    self_both = same_rows[:, None, :, None] & same_cols[None, :, None, :]
    return (near_both, self_both)

def window_part(queries, key_region, value_region, permitted_mask, group_size):
    head_dimension = queries.shape[-1] // HEAD_COUNT
    scale = 1.0 / math.sqrt(head_dimension)
    numerators, maxima, totals = ([], [], [])
    for head_first in range(0, HEAD_COUNT, group_size):
        lower = head_first * head_dimension
        upper = (head_first + group_size) * head_dimension
        query_grp = queries[:, lower:upper].reshape(queries.shape[0], group_size, head_dimension).astype(jnp.float32)
        key_grp = key_region[:, lower:upper].reshape(key_region.shape[0], group_size, head_dimension).astype(jnp.float32)
        value_grp = value_region[:, lower:upper].reshape(value_region.shape[0], group_size, head_dimension).astype(jnp.float32)
        scores = jnp.einsum('qhd,khd->hqk', query_grp, key_grp) * scale
        scores = jnp.where(permitted_mask[None], scores, NEG_FILL)
        highest = lax.optimization_barrier(jnp.max(scores, axis=-1))
        exp_terms = jnp.exp(scores - highest[..., None])
        totals.append(lax.optimization_barrier(jnp.sum(exp_terms, axis=-1)))
        rounded = lax.optimization_barrier(exp_terms.astype(jnp.bfloat16))
        numerators.append(jnp.einsum('hqk,khd->qhd', rounded.astype(jnp.float32), value_grp))
        maxima.append(highest)
    return (jnp.concatenate(numerators, axis=1), jnp.concatenate(maxima, axis=0).T, jnp.concatenate(totals, axis=0).T)

def dilation_valid_mask(tissue, row_indices, head_indices, column_indices, dilation_levels, segment_levels, selected_count, column_total):
    key_columns = jnp.arange(selected_count, dtype=jnp.int32)[None, :] * DILATION_MIN + (head_indices % DILATION_MIN)[:, None]
    tissue_keys = tissue[row_indices[:, None], key_columns]
    dilation_stride = jnp.left_shift(jnp.int32(DILATION_MIN), dilation_levels[head_indices])
    segment = jnp.right_shift(jnp.int32(column_total), segment_levels[head_indices])
    phase_ok = key_columns % dilation_stride[:, None] == (head_indices % dilation_stride)[:, None]
    key_seg = key_columns // segment[:, None]
    query_seg = column_indices[None, :] // segment[:, None]
    same_seg = key_seg[:, None, :] == query_seg[:, :, None]
    return same_seg & ((tissue_keys == 1) & phase_ok)[:, None, :]

def dilation_partial(queries, keys_sel, values_sel, permitted_mask):
    scale = 1.0 / math.sqrt(queries.shape[-1])
    scores = jnp.einsum('icw,isw->ics', queries.astype(jnp.float32), keys_sel.astype(jnp.float32)) * scale
    scores = jnp.where(permitted_mask, scores, NEG_FILL)
    highest = lax.optimization_barrier(jnp.max(scores, axis=-1))
    exp_terms = jnp.where(permitted_mask, jnp.exp(scores - highest[..., None]), 0.0)
    totals = lax.optimization_barrier(jnp.sum(exp_terms, axis=-1))
    rounded = lax.optimization_barrier(exp_terms.astype(jnp.bfloat16))
    softmax_numer = jnp.einsum('ics,isw->icw', rounded.astype(jnp.float32), values_sel.astype(jnp.float32))
    return (softmax_numer, highest, totals)

def merge_partials(neighbour_numer, neighbour_max, neighbour_sum, dilation_numer, dilation_score_max, dilation_sum):
    running_maximum = jnp.maximum(neighbour_max, dilation_score_max)
    neighbour_rescale = jnp.exp(neighbour_max - running_maximum)
    dilation_rescale = jnp.exp(dilation_score_max - running_maximum)
    softmax_numer = neighbour_rescale[..., None] * neighbour_numer + dilation_rescale[..., None] * dilation_numer
    softmax_denom = neighbour_rescale * neighbour_sum + dilation_rescale * dilation_sum
    return softmax_numer / softmax_denom[..., None]

def reference(query_matrix, key_matrix, value_matrix, tissue, dilation_levels, segment_levels, output_matrix):
    head_dimension = D // HEAD_COUNT
    column_shifts = np.arange(HEAD_COUNT) % DILATION_MIN
    head_sequence = np.arange(HEAD_COUNT)
    key_selected = key_matrix.reshape(GRID_ROWS, GRID_COLUMNS // DILATION_MIN, DILATION_MIN, HEAD_COUNT, head_dimension)[:, :, column_shifts, head_sequence]
    value_selected = value_matrix.reshape(GRID_ROWS, GRID_COLUMNS // DILATION_MIN, DILATION_MIN, HEAD_COUNT, head_dimension)[:, :, column_shifts, head_sequence]
    head_indices = jnp.arange(HEAD_COUNT, dtype=jnp.int32)
    column_indices = jnp.arange(GRID_COLUMNS, dtype=jnp.int32)

    def single_row(row_position):
        q_row = lax.dynamic_index_in_dim(query_matrix, row_position, 0, keepdims=False).reshape(GRID_COLUMNS, HEAD_COUNT, head_dimension).transpose(1, 0, 2)
        k_row = lax.dynamic_index_in_dim(key_selected, row_position, 0, keepdims=False).transpose(1, 0, 2)
        v_row = lax.dynamic_index_in_dim(value_selected, row_position, 0, keepdims=False).transpose(1, 0, 2)
        permitted_mask = dilation_valid_mask(tissue, jnp.full((HEAD_COUNT,), row_position, jnp.int32), head_indices, column_indices, dilation_levels, segment_levels, REACHED_TILES, GRID_COLUMNS)
        softmax_numer, highest, totals = dilation_partial(q_row, k_row, v_row, permitted_mask)
        return (softmax_numer.transpose(1, 0, 2), highest.T, totals.T)
    dilation_numer, dilation_score_max, dilation_sum = lax.map(single_row, jnp.arange(GRID_ROWS, dtype=jnp.int32))
    k_pad = jnp.pad(key_matrix, ((R, R), (R, R), (0, 0)))
    v_pad = jnp.pad(value_matrix, ((R, R), (R, R), (0, 0)))
    tissue_pad = jnp.pad(tissue, R)
    near_both, self_both = window_static(DEVICE_GRID_ROWS, DEVICE_GRID_COLS)
    zero_index = jnp.zeros((), jnp.int32)

    def one_block(block_id):
        row_offset = block_id // N_COL * DEVICE_GRID_ROWS
        column_offset = block_id % N_COL * DEVICE_GRID_COLS
        key_region = lax.dynamic_slice(k_pad, (row_offset, column_offset, zero_index), (DEVICE_GRID_ROWS + 2 * R, DEVICE_GRID_COLS + 2 * R, D)).reshape(-1, D)
        value_region = lax.dynamic_slice(v_pad, (row_offset, column_offset, zero_index), (DEVICE_GRID_ROWS + 2 * R, DEVICE_GRID_COLS + 2 * R, D)).reshape(-1, D)
        tissue_reg = lax.dynamic_slice(tissue_pad, (row_offset, column_offset), (DEVICE_GRID_ROWS + 2 * R, DEVICE_GRID_COLS + 2 * R))
        permitted_mask = jnp.asarray(near_both) & (tissue_reg[None, None] == 1) | jnp.asarray(self_both)
        permitted_mask = permitted_mask.reshape(DEVICE_GRID_ROWS * DEVICE_GRID_COLS, -1)
        queries = lax.dynamic_slice(query_matrix, (row_offset, column_offset, zero_index), (DEVICE_GRID_ROWS, DEVICE_GRID_COLS, D)).reshape(-1, D)
        neighbour_numer, neighbour_max, neighbour_sum = window_part(queries, key_region, value_region, permitted_mask, 2)
        local_block_numer = lax.dynamic_slice(dilation_numer, (row_offset, column_offset, zero_index, zero_index), (DEVICE_GRID_ROWS, DEVICE_GRID_COLS, HEAD_COUNT, head_dimension)).reshape(-1, HEAD_COUNT, head_dimension)
        local_block_max = lax.dynamic_slice(dilation_score_max, (row_offset, column_offset, zero_index), (DEVICE_GRID_ROWS, DEVICE_GRID_COLS, HEAD_COUNT)).reshape(-1, HEAD_COUNT)
        local_block_sum = lax.dynamic_slice(dilation_sum, (row_offset, column_offset, zero_index), (DEVICE_GRID_ROWS, DEVICE_GRID_COLS, HEAD_COUNT)).reshape(-1, HEAD_COUNT)
        attended = merge_partials(neighbour_numer, neighbour_max, neighbour_sum, local_block_numer, local_block_max, local_block_sum).reshape(-1, D).astype(jnp.bfloat16)
        encoded = jnp.dot(attended, output_matrix, preferred_element_type=jnp.float32).astype(jnp.bfloat16)
        return encoded.reshape(DEVICE_GRID_ROWS, DEVICE_GRID_COLS, D)
    blocks = lax.map(one_block, jnp.arange(N_ROW * N_COL, dtype=jnp.int32))
    return blocks.reshape(N_ROW, N_COL, DEVICE_GRID_ROWS, DEVICE_GRID_COLS, D).transpose(0, 2, 1, 3, 4).reshape(GRID_ROWS, GRID_COLUMNS, D)
```

```python
import functools
import math

import jax
import jax.numpy as jnp
from jax import lax
from jax.experimental import pallas as pl
from jax.experimental.pallas import tpu as pltpu
from jax.sharding import PartitionSpec as P

HEAD_COUNT = 16
R = 8
DILATION_MIN = 8
NEG_FILL = -1e30
MESH = pl.DeviceIdType.MESH
HEADS_TOGETHER = 4
F32 = jnp.float32
BF16 = jnp.bfloat16


def iota(shape, dim):
    return lax.broadcasted_iota(jnp.int32, shape, dim)


def one_hot(condition):
    return jnp.where(condition, 1.0, 0.0).astype(BF16)


def lane_window(group, head_dimension):
    first = group * HEADS_TOGETHER * head_dimension
    return first // 128 * 128, first % 128


def head_mask(group, head, head_dimension):
    _, offset = lane_window(group, head_dimension)
    lane = iota((1, 256), 1) - offset - head * head_dimension
    return (lane >= 0) & (lane < head_dimension)


def gathered_tissue(tissue, key_rows, key_cols):
    rows, cols = tissue.shape
    n = key_rows.shape[1]
    pick = one_hot(iota((cols, n), 0) == key_cols)
    by_col = jnp.dot(tissue, pick, preferred_element_type=F32)
    keep = iota((rows, n), 0) == key_rows
    return jnp.sum(jnp.where(keep, by_col, 0.0), axis=0, keepdims=True)


def window_bias(tissue, key_rel_row, key_rel_col, row_offset, column_offset, dr, dc):
    present = gathered_tissue(tissue, key_rel_row + row_offset, key_rel_col + column_offset)
    n = key_rel_row.shape[1]
    q = iota((dr * dc, n), 0)
    row_gap = jnp.abs(key_rel_row - q // dc)
    col_gap = jnp.abs(key_rel_col - q % dc)
    near = (row_gap <= R) & (col_gap <= R) & (present > 0.5)
    self_key = (row_gap + col_gap) == 0
    return jnp.where(near | self_key, 0.0, NEG_FILL)


def kernel(
    n_row, n_col, dr, dc,
    q_hbm, k_hbm, v_hbm, tissue_ref, dil_ref, seg_ref, w_hbm, out_ref,
    q_ref, w_ref, near_kv, far_kv, halves, chosen, bias_a, bias_b, tissue_dil,
    num_a, max_a, sum_a, local_sem, send_sem, recv_sem, dil_send, dil_recv,
):
    row, col = lax.axis_index("row"), lax.axis_index("col")
    tiles, width = q_ref.shape
    hd = width // HEAD_COUNT
    half = tiles // 2
    win_far = 6 * half
    sel = tiles // DILATION_MIN

    loads = [
        pltpu.make_async_copy(k_hbm, near_kv.at[0, pl.ds(0, tiles)], local_sem.at[0]),
        pltpu.make_async_copy(v_hbm, near_kv.at[1, pl.ds(0, tiles)], local_sem.at[1]),
        pltpu.make_async_copy(q_hbm, q_ref, local_sem.at[2]),
        pltpu.make_async_copy(w_hbm, w_ref, local_sem.at[3]),
    ]
    for load in loads:
        load.start()

    has_up, has_down = row > 0, row < n_row - 1
    has_left, has_right = col > 0, col < n_col - 1
    up = (lax.rem(row + n_row - 1, n_row), col)
    down = (lax.rem(row + 1, n_row), col)
    left = (row, lax.rem(col + n_col - 1, n_col))
    right = (row, lax.rem(col + 1, n_col))

    barrier = pltpu.get_barrier_semaphore()

    @pl.when(has_up)
    def _():
        pl.semaphore_signal(barrier, inc=1, device_id=up, device_id_type=MESH)

    @pl.when(has_down)
    def _():
        pl.semaphore_signal(barrier, inc=1, device_id=down, device_id_type=MESH)

    for d in range(1, n_col):
        peer = (row, lax.rem(col + d, n_col))
        pl.semaphore_signal(barrier, inc=1, device_id=peer, device_id_type=MESH)

    def remote(src, dst, kind, device):
        return pltpu.make_async_remote_copy(
            src_ref=src, dst_ref=dst, send_sem=send_sem.at[kind], recv_sem=recv_sem.at[kind],
            device_id=device, device_id_type=MESH,
        )

    def near_rows(first, count):
        return near_kv.at[:, pl.ds(first, count)]

    def far_rows(first, count):
        return far_kv.at[:, pl.ds(first, count)]

    own = near_rows(0, tiles)
    to_up = remote(own, near_rows(2 * tiles, tiles), 0, up)
    to_down = remote(own, near_rows(tiles, tiles), 1, down)
    to_left = remote(halves.at[:, pl.ds(0, half)], far_rows(half, half), 2, left)
    to_right = remote(halves.at[:, pl.ds(half, half)], far_rows(0, half), 3, right)
    left_to_up = remote(far_rows(0, half), far_rows(4 * half, half), 4, up)
    left_to_down = remote(far_rows(0, half), far_rows(2 * half, half), 5, down)
    right_to_up = remote(far_rows(half, half), far_rows(5 * half, half), 6, up)
    right_to_down = remote(far_rows(half, half), far_rows(3 * half, half), 7, down)

    i, j = iota((tiles, tiles), 0), iota((tiles, tiles), 1)
    within = i % half
    split_order = one_hot(j == within // R * dc + (i // half) * R + within % R)
    local_sel = dc // DILATION_MIN
    s = i % sel
    phase_order = one_hot(j == s // local_sel * dc + s % local_sel * DILATION_MIN + i // sel)
    lane_phase = iota((1, width), 1) // hd % DILATION_MIN
    slot = pl.ds(pl.multiple_of(win_far + col * sel, sel), sel)

    loads[0].wait()
    loads[1].wait()
    for t in range(2):
        mine = near_kv[t, pl.ds(0, tiles)]
        halves[t] = jnp.dot(split_order, mine, preferred_element_type=F32).astype(BF16)
    pl.semaphore_wait(
        barrier,
        (n_col - 1) + jnp.where(has_up, 1, 0) + jnp.where(has_down, 1, 0),
    )
    pl.when(has_left)(to_left.start)
    pl.when(has_right)(to_right.start)
    pl.when(has_up)(to_up.start)
    pl.when(has_down)(to_down.start)
    for t in range(2):
        mine = near_kv[t, pl.ds(0, tiles)]
        by_phase = jnp.dot(phase_order, mine, preferred_element_type=F32)
        picked = jnp.zeros((sel, width), F32)
        for p in range(DILATION_MIN):
            picked += jnp.where(lane_phase == p, by_phase[p * sel:(p + 1) * sel], 0.0)
        picked = picked.astype(BF16)
        chosen[t] = picked
        far_kv[t, slot] = picked
    dil = []
    for d in range(1, n_col):
        copy = pltpu.make_async_remote_copy(
            src_ref=chosen, dst_ref=far_kv.at[:, slot],
            send_sem=dil_send.at[d], recv_sem=dil_recv.at[d],
            device_id=(row, lax.rem(col + d, n_col)), device_id_type=MESH,
        )
        copy.start()
        dil.append(copy)

    def clear_near(first):
        near_kv[:, pl.ds(first, tiles)] = jnp.zeros((2, tiles, width), BF16)

    def clear_far(first):
        far_kv[:, pl.ds(first, half)] = jnp.zeros((2, half, width), BF16)

    @pl.when(jnp.logical_not(has_up))
    def _():
        clear_near(tiles)

    @pl.when(jnp.logical_not(has_down))
    def _():
        clear_near(2 * tiles)

    for side, has_side in ((0, has_left), (1, has_right)):
        for block, has_block in ((0, None), (1, has_up), (2, has_down)):
            have = has_side if has_block is None else has_side & has_block

            @pl.when(jnp.logical_not(have))
            def _(side=side, block=block):
                clear_far((2 * block + side) * half)

    tissue = tissue_ref[...].astype(F32).astype(BF16)
    row_offset, column_offset = row * dr, col * dc
    k = iota((1, 3 * tiles), 1)
    block = k // tiles
    shift = jnp.where(block == 1, -dr, jnp.where(block == 2, dr, 0))
    inner = k % tiles
    bias_a[...] = window_bias(
        tissue, inner // dc + shift, inner % dc, row_offset, column_offset, dr, dc
    )
    within = inner % half
    far_col = jnp.where(inner >= half, dc, -R) + within % R
    bias_b[...] = window_bias(
        tissue, within // R + shift, far_col, row_offset, column_offset, dr, dc
    )
    n_dil = sel * n_col
    kd = iota((1, n_dil), 1)
    dil_row = kd % sel // local_sel
    dil_col = kd // sel * dc + kd % local_sel * DILATION_MIN
    for p in range(DILATION_MIN):
        tissue_dil[pl.ds(p, 1)] = gathered_tissue(tissue, dil_row + row_offset, dil_col + p)

    @pl.when(has_left)
    def _():
        to_right.wait_recv()
        pl.when(has_up)(left_to_up.start)
        pl.when(has_down)(left_to_down.start)

    @pl.when(has_right)
    def _():
        to_left.wait_recv()
        pl.when(has_up)(right_to_up.start)
        pl.when(has_down)(right_to_down.start)

    pl.when(has_down)(to_up.wait_recv)
    pl.when(has_up)(to_down.wait_recv)
    loads[2].wait()

    factor = math.log2(math.e) / math.sqrt(hd)
    groups = HEAD_COUNT // HEADS_TOGETHER
    stacked = HEADS_TOGETHER * tiles

    def stacked_queries(g):
        base, _ = lane_window(g, hd)
        query = q_ref[:, pl.ds(base, 256)]
        return jnp.concatenate(
            [
                jnp.where(head_mask(g, h, hd), query, jnp.zeros_like(query))
                for h in range(HEADS_TOGETHER)
            ],
            axis=0,
        )

    def scores(g, kv, first, count):
        base, _ = lane_window(g, hd)
        keys = kv[0, pl.ds(first, count), pl.ds(base, 256)]
        raw = lax.dot_general(
            stacked_queries(g), keys, (((1,), (1,)), ((), ())), preferred_element_type=F32
        )
        return raw.reshape(HEADS_TOGETHER, tiles, count)

    for g in range(groups):
        base, _ = lane_window(g, hd)
        s = scores(g, near_kv, 0, 3 * tiles) + bias_a[...][None]
        top = jnp.max(s, axis=-1, keepdims=True)
        p = jnp.exp2((s - top) * factor)
        max_a[g] = top.reshape(stacked, 1)
        sum_a[g] = jnp.sum(p, axis=-1, keepdims=True).reshape(stacked, 1)
        num_a[g] = jnp.dot(
            p.astype(BF16).reshape(stacked, 3 * tiles),
            near_kv[1, :, pl.ds(base, 256)],
            preferred_element_type=F32,
        )

    q_idx = iota((tiles, n_dil), 0)
    q_col = column_offset + q_idx % dc
    same_row = dil_row == q_idx // dc
    for copy in dil:
        copy.wait_recv()

    @pl.when(has_left)
    def _():
        pl.when(has_up)(left_to_down.wait_recv)
        pl.when(has_down)(left_to_up.wait_recv)

    @pl.when(has_right)
    def _():
        pl.when(has_up)(right_to_down.wait_recv)
        pl.when(has_down)(right_to_up.wait_recv)

    parts = []
    for g in range(groups):
        base, _ = lane_window(g, hd)
        s_win = scores(g, far_kv, 0, win_far) + bias_b[...][None]
        s_dil = scores(g, far_kv, win_far, n_dil)
        masked = []
        for h in range(HEADS_TOGETHER):
            head = g * HEADS_TOGETHER + h
            stride = jnp.left_shift(jnp.int32(DILATION_MIN), dil_ref[head])
            segment = jnp.right_shift(jnp.int32(dc * n_col), seg_ref[head])
            key_col = dil_col + head % DILATION_MIN
            present = tissue_dil[pl.ds(head % DILATION_MIN, 1)] > 0.5
            key_ok = present & ((key_col & (stride - 1)) == (head & (stride - 1)))
            ok = key_ok & same_row & ((key_col ^ q_col) < segment)
            masked.append(jnp.where(ok, s_dil[h], NEG_FILL)[None])
        s_dil = jnp.concatenate(masked, axis=0)
        old_top = max_a[g].reshape(HEADS_TOGETHER, tiles, 1)
        top = jnp.maximum(
            jnp.maximum(
                jnp.max(s_win, axis=-1, keepdims=True), jnp.max(s_dil, axis=-1, keepdims=True)
            ),
            old_top,
        )
        p_win = jnp.exp2((s_win - top) * factor)
        p_dil = jnp.exp2((s_dil - top) * factor)
        keep = jnp.exp2((old_top - top) * factor).reshape(stacked, 1)
        total = (
            keep * sum_a[g]
            + jnp.sum(p_win, axis=-1, keepdims=True).reshape(stacked, 1)
            + jnp.sum(p_dil, axis=-1, keepdims=True).reshape(stacked, 1)
        )
        numer = (
            keep * num_a[g]
            + jnp.dot(
                p_win.astype(BF16).reshape(stacked, win_far),
                far_kv[1, pl.ds(0, win_far), pl.ds(base, 256)],
                preferred_element_type=F32,
            )
            + jnp.dot(
                p_dil.astype(BF16).reshape(stacked, n_dil),
                far_kv[1, pl.ds(win_far, n_dil), pl.ds(base, 256)],
                preferred_element_type=F32,
            )
        )
        mixed = numer / total
        together = jnp.zeros((tiles, 256), F32)
        for h in range(HEADS_TOGETHER):
            together += jnp.where(
                head_mask(g, h, hd), mixed[h * tiles:(h + 1) * tiles], 0.0
            )
        parts.append(together)

    lanes = []
    for g in range(0, groups, 2):
        a, b = parts[g], parts[g + 1]
        lanes += [a[:, :128], a[:, 128:] + b[:, :128], b[:, 128:]]
    attended = jnp.concatenate(lanes, axis=1).astype(BF16)
    loads[3].wait()
    out_ref[...] = jnp.dot(attended, w_ref[...], preferred_element_type=F32).astype(BF16)

    pl.when(has_left)(to_left.wait_send)
    pl.when(has_right)(to_right.wait_send)
    pl.when(has_up)(to_up.wait_send)
    pl.when(has_down)(to_down.wait_send)
    pl.when(has_left & has_up)(left_to_up.wait_send)
    pl.when(has_left & has_down)(left_to_down.wait_send)
    pl.when(has_right & has_up)(right_to_up.wait_send)
    pl.when(has_right & has_down)(right_to_down.wait_send)
    for copy in dil:
        copy.wait_send()


def solution(mesh):
    n_row, n_col = mesh.shape["row"], mesh.shape["col"]

    def per_device(q, k, v, tissue, dilation_levels, segment_levels, output_matrix):
        dr, dc, width = q.shape
        tiles = dr * dc
        sel = tiles // DILATION_MIN
        groups = HEAD_COUNT // HEADS_TOGETHER
        stacked = HEADS_TOGETHER * tiles
        any_space = pl.BlockSpec(memory_space=pl.ANY)
        vmem = pl.BlockSpec(memory_space=pltpu.VMEM)
        smem = pl.BlockSpec(memory_space=pltpu.SMEM)
        out = pl.pallas_call(
            functools.partial(kernel, n_row, n_col, dr, dc),
            out_shape=jax.ShapeDtypeStruct((tiles, width), BF16),
            in_specs=[any_space, any_space, any_space, vmem, smem, smem, any_space],
            out_specs=vmem,
            scratch_shapes=[
                pltpu.VMEM((tiles, width), BF16),
                pltpu.VMEM(output_matrix.shape, BF16),
                pltpu.VMEM((2, 3 * tiles, width), BF16),
                pltpu.VMEM((2, 3 * tiles + sel * n_col, width), BF16),
                pltpu.VMEM((2, tiles, width), BF16),
                pltpu.VMEM((2, sel, width), BF16),
                pltpu.VMEM((tiles, 3 * tiles), F32),
                pltpu.VMEM((tiles, 3 * tiles), F32),
                pltpu.VMEM((DILATION_MIN, sel * n_col), F32),
                pltpu.VMEM((groups, stacked, 256), F32),
                pltpu.VMEM((groups, stacked, 1), F32),
                pltpu.VMEM((groups, stacked, 1), F32),
                pltpu.SemaphoreType.DMA((4,)),
                pltpu.SemaphoreType.DMA((8,)),
                pltpu.SemaphoreType.DMA((8,)),
                pltpu.SemaphoreType.DMA((n_col,)),
                pltpu.SemaphoreType.DMA((n_col,)),
            ],
            compiler_params=pltpu.CompilerParams(
                collective_id=0, has_side_effects=True, vmem_limit_bytes=56 * 1024 * 1024
            ),
        )(
            q.reshape(tiles, width), k.reshape(tiles, width), v.reshape(tiles, width),
            tissue, dilation_levels, segment_levels, output_matrix,
        )
        return out.reshape(dr, dc, width)

    split = P("row", "col", None)
    return jax.shard_map(
        per_device,
        mesh=mesh,
        in_specs=(split, split, split, P(), P(), P(), P()),
        out_specs=split,
        check_vma=False,
    )
```

```python
import functools
import math

import jax
import jax.numpy as jnp
from jax import lax
from jax.experimental import pallas as pl
from jax.experimental.pallas import tpu as pltpu
from jax.sharding import PartitionSpec as P

HEAD_COUNT = 16
R = 8
DILATION_MIN = 8
NEG_FILL = -1e30
MESH = pl.DeviceIdType.MESH
HEADS_TOGETHER = 4
F32 = jnp.float32
BF16 = jnp.bfloat16


def iota(shape, dim):
    return lax.broadcasted_iota(jnp.int32, shape, dim)


def one_hot(condition):
    return jnp.where(condition, 1.0, 0.0).astype(BF16)


def lane_window(group, head_dimension):
    first = group * HEADS_TOGETHER * head_dimension
    return first // 128 * 128, first % 128


def head_mask(group, head, head_dimension):
    _, offset = lane_window(group, head_dimension)
    lane = iota((1, 256), 1) - offset - head * head_dimension
    return (lane >= 0) & (lane < head_dimension)


def gathered_tissue(tissue, key_rows, key_cols):
    rows, cols = tissue.shape
    n = key_rows.shape[1]
    pick = one_hot(iota((cols, n), 0) == key_cols)
    by_col = jnp.dot(tissue, pick, preferred_element_type=F32)
    keep = iota((rows, n), 0) == key_rows
    return jnp.sum(jnp.where(keep, by_col, 0.0), axis=0, keepdims=True)


def window_bias(tissue, key_rel_row, key_rel_col, row_offset, column_offset, dr, dc):
    present = gathered_tissue(tissue, key_rel_row + row_offset, key_rel_col + column_offset)
    n = key_rel_row.shape[1]
    q = iota((dr * dc, n), 0)
    row_gap = jnp.abs(key_rel_row - q // dc)
    col_gap = jnp.abs(key_rel_col - q % dc)
    near = (row_gap <= R) & (col_gap <= R) & (present > 0.5)
    self_key = (row_gap + col_gap) == 0
    return jnp.where(near | self_key, 0.0, NEG_FILL)


def kernel(
    n_row, n_col, dr, dc,
    q_hbm, k_hbm, v_hbm, tissue_ref, dil_ref, seg_ref, out_ref,
    q_ref, own_kv, mid_kv, far_kv, halves, chosen, bias_own, bias_mid, bias_far,
    numer, highest, total, local_sem, send_sem, recv_sem, dil_send, dil_recv,
):
    row, col = lax.axis_index("row"), lax.axis_index("col")
    tiles, width = q_ref.shape
    hd = width // HEAD_COUNT
    half = tiles // 2
    corners = 4 * half
    sel = tiles // DILATION_MIN

    loads = [
        pltpu.make_async_copy(k_hbm, own_kv.at[0], local_sem.at[0]),
        pltpu.make_async_copy(v_hbm, own_kv.at[1], local_sem.at[1]),
        pltpu.make_async_copy(q_hbm, q_ref, local_sem.at[2]),
    ]
    for load in loads:
        load.start()

    has_up, has_down = row > 0, row < n_row - 1
    has_left, has_right = col > 0, col < n_col - 1
    up = (lax.rem(row + n_row - 1, n_row), col)
    down = (lax.rem(row + 1, n_row), col)
    left = (row, lax.rem(col + n_col - 1, n_col))
    right = (row, lax.rem(col + 1, n_col))

    barrier = pltpu.get_barrier_semaphore()

    @pl.when(has_up)
    def _():
        pl.semaphore_signal(barrier, inc=1, device_id=up, device_id_type=MESH)

    @pl.when(has_down)
    def _():
        pl.semaphore_signal(barrier, inc=1, device_id=down, device_id_type=MESH)

    for d in range(1, n_col):
        peer = (row, lax.rem(col + d, n_col))
        pl.semaphore_signal(barrier, inc=1, device_id=peer, device_id_type=MESH)

    def remote(src, dst, kind, device):
        return pltpu.make_async_remote_copy(
            src_ref=src, dst_ref=dst, send_sem=send_sem.at[kind], recv_sem=recv_sem.at[kind],
            device_id=device, device_id_type=MESH,
        )

    def mid(first, count):
        return mid_kv.at[:, pl.ds(first, count)]

    def corner(index):
        return far_kv.at[:, pl.ds(index * half, half)]

    left_here, right_here = mid(2 * tiles, half), mid(2 * tiles + half, half)
    to_up = remote(own_kv, mid(tiles, tiles), 0, up)
    to_down = remote(own_kv, mid(0, tiles), 1, down)
    to_left = remote(halves.at[:, pl.ds(0, half)], right_here, 2, left)
    to_right = remote(halves.at[:, pl.ds(half, half)], left_here, 3, right)
    left_to_up = remote(left_here, corner(2), 4, up)
    left_to_down = remote(left_here, corner(0), 5, down)
    right_to_up = remote(right_here, corner(3), 6, up)
    right_to_down = remote(right_here, corner(1), 7, down)

    i, j = iota((tiles, tiles), 0), iota((tiles, tiles), 1)
    within = i % half
    split_order = one_hot(j == within // R * dc + (i // half) * R + within % R)
    local_sel = dc // DILATION_MIN
    s = i % sel
    phase_order = one_hot(j == s // local_sel * dc + s % local_sel * DILATION_MIN + i // sel)
    lane_phase = iota((1, width), 1) // hd % DILATION_MIN
    slot = pl.ds(pl.multiple_of(corners + col * sel, sel), sel)

    loads[0].wait()
    loads[1].wait()
    for t in range(2):
        halves[t] = jnp.dot(split_order, own_kv[t], preferred_element_type=F32).astype(BF16)
    pl.semaphore_wait(
        barrier,
        (n_col - 1) + jnp.where(has_up, 1, 0) + jnp.where(has_down, 1, 0),
    )
    pl.when(has_left)(to_left.start)
    pl.when(has_right)(to_right.start)
    pl.when(has_up)(to_up.start)
    pl.when(has_down)(to_down.start)
    for t in range(2):
        by_phase = jnp.dot(phase_order, own_kv[t], preferred_element_type=F32)
        picked = jnp.zeros((sel, width), F32)
        for p in range(DILATION_MIN):
            picked += jnp.where(lane_phase == p, by_phase[p * sel:(p + 1) * sel], 0.0)
        picked = picked.astype(BF16)
        chosen[t] = picked
        far_kv[t, slot] = picked
    dil = []
    for d in range(1, n_col):
        copy = pltpu.make_async_remote_copy(
            src_ref=chosen, dst_ref=far_kv.at[:, slot],
            send_sem=dil_send.at[d], recv_sem=dil_recv.at[d],
            device_id=(row, lax.rem(col + d, n_col)), device_id_type=MESH,
        )
        copy.start()
        dil.append(copy)

    def clear(ref, first, count):
        ref[:, pl.ds(first, count)] = jnp.zeros((2, count, width), BF16)

    for ref, first, count, have in (
        (mid_kv, 0, tiles, has_up),
        (mid_kv, tiles, tiles, has_down),
        (mid_kv, 2 * tiles, half, has_left),
        (mid_kv, 2 * tiles + half, half, has_right),
        (far_kv, 0, half, has_up & has_left),
        (far_kv, half, half, has_up & has_right),
        (far_kv, 2 * half, half, has_down & has_left),
        (far_kv, 3 * half, half, has_down & has_right),
    ):
        pl.when(jnp.logical_not(have))(functools.partial(clear, ref, first, count))

    tissue = tissue_ref[...].astype(F32).astype(BF16)
    row_offset, column_offset = row * dr, col * dc

    def bias(key_row, key_col):
        return window_bias(tissue, key_row, key_col, row_offset, column_offset, dr, dc)

    def half_col(k):
        return jnp.where(k % tiles >= half, dc, -R) + k % R

    k = iota((1, tiles), 1)
    bias_own[...] = bias(k // dc, k % dc)
    for block, shift in ((0, -dr), (1, dr)):
        bias_mid[:, pl.ds(block * tiles, tiles)] = bias(k // dc + shift, k % dc)
    bias_mid[:, pl.ds(2 * tiles, tiles)] = bias(k % half // R, half_col(k))

    factor = math.log2(math.e) / math.sqrt(hd)
    groups = HEAD_COUNT // HEADS_TOGETHER
    stacked = HEADS_TOGETHER * tiles

    def attend(g, kv, extra, before):
        base, _ = lane_window(g, hd)
        query = q_ref[:, pl.ds(base, 256)]
        query = jnp.concatenate(
            [
                jnp.where(head_mask(g, h, hd), query, jnp.zeros_like(query))
                for h in range(HEADS_TOGETHER)
            ],
            axis=0,
        )
        scores = lax.dot_general(
            query, kv[0, :, pl.ds(base, 256)], (((1,), (1,)), ((), ())),
            preferred_element_type=F32,
        )
        scores = scores.reshape(HEADS_TOGETHER, tiles, kv.shape[1]) + extra
        scores = scores.reshape(stacked, kv.shape[1])
        top = jnp.max(scores, axis=-1, keepdims=True)
        if before is not None:
            old_numer, old_top, old_total = before
            top = jnp.maximum(top, old_top)
        probs = jnp.exp2((scores - top) * factor)
        new_total = jnp.sum(probs, axis=-1, keepdims=True)
        new_numer = jnp.dot(
            probs.astype(BF16), kv[1, :, pl.ds(base, 256)], preferred_element_type=F32
        )
        if before is not None:
            keep = jnp.exp2((old_top - top) * factor)
            new_total += keep * old_total
            new_numer += keep * old_numer
        return new_numer, top, new_total

    loads[2].wait()
    for g in range(groups):
        numer[g], highest[g], total[g] = attend(g, own_kv, bias_own[...][None], None)

    @pl.when(has_left)
    def _():
        to_right.wait_recv()
        pl.when(has_up)(left_to_up.start)
        pl.when(has_down)(left_to_down.start)

    @pl.when(has_right)
    def _():
        to_left.wait_recv()
        pl.when(has_up)(right_to_up.start)
        pl.when(has_down)(right_to_down.start)

    for block, shift in ((0, -dr), (1, dr)):
        bias_far[0, :, pl.ds(block * tiles, tiles)] = bias(k % half // R + shift, half_col(k))
    for h in range(1, HEAD_COUNT):
        bias_far[h, :, pl.ds(0, corners)] = bias_far[0, :, pl.ds(0, corners)]
    n_dil = sel * n_col
    kd = iota((1, n_dil), 1)
    dil_row = kd % sel // local_sel
    dil_col = kd // sel * dc + kd % local_sel * DILATION_MIN
    q_idx = iota((tiles, n_dil), 0)
    q_col = column_offset + q_idx % dc
    same_row = dil_row == q_idx // dc
    for p in range(DILATION_MIN):
        key_col = dil_col + p
        present = gathered_tissue(tissue, dil_row + row_offset, key_col) > 0.5
        apart = key_col ^ q_col
        for head in range(p, HEAD_COUNT, DILATION_MIN):
            stride = jnp.left_shift(jnp.int32(DILATION_MIN), dil_ref[head])
            segment = jnp.right_shift(jnp.int32(dc * n_col), seg_ref[head])
            key_ok = present & ((key_col & (stride - 1)) == (head & (stride - 1)))
            ok = key_ok & same_row & (apart < segment)
            bias_far[head, :, pl.ds(corners, n_dil)] = jnp.where(ok, 0.0, NEG_FILL)

    pl.when(has_down)(to_up.wait_recv)
    pl.when(has_up)(to_down.wait_recv)
    for g in range(groups):
        numer[g], highest[g], total[g] = attend(
            g, mid_kv, bias_mid[...][None], (numer[g], highest[g], total[g])
        )

    for copy in dil:
        copy.wait_recv()

    @pl.when(has_left)
    def _():
        pl.when(has_up)(left_to_down.wait_recv)
        pl.when(has_down)(left_to_up.wait_recv)

    @pl.when(has_right)
    def _():
        pl.when(has_up)(right_to_down.wait_recv)
        pl.when(has_down)(right_to_up.wait_recv)

    parts = []
    for g in range(groups):
        heads = pl.ds(g * HEADS_TOGETHER, HEADS_TOGETHER)
        top_numer, _, top_total = attend(
            g, far_kv, bias_far[heads], (numer[g], highest[g], total[g])
        )
        mixed = top_numer * (1.0 / top_total)
        together = jnp.zeros((tiles, 256), F32)
        for h in range(HEADS_TOGETHER):
            together = jnp.where(head_mask(g, h, hd), mixed[h * tiles:(h + 1) * tiles], together)
        parts.append(together)
    for g in range(0, groups, 2):
        a, b = parts[g], parts[g + 1]
        lanes = [a[:, :128], a[:, 128:] + b[:, :128], b[:, 128:]]
        attended = jnp.concatenate(lanes, axis=1).astype(BF16)
        out_ref[:, pl.ds(g // 2 * 384, 384)] = attended

    pl.when(has_left)(to_left.wait_send)
    pl.when(has_right)(to_right.wait_send)
    pl.when(has_up)(to_up.wait_send)
    pl.when(has_down)(to_down.wait_send)
    pl.when(has_left & has_up)(left_to_up.wait_send)
    pl.when(has_left & has_down)(left_to_down.wait_send)
    pl.when(has_right & has_up)(right_to_up.wait_send)
    pl.when(has_right & has_down)(right_to_down.wait_send)
    for copy in dil:
        copy.wait_send()


def solution(mesh):
    n_row, n_col = mesh.shape["row"], mesh.shape["col"]

    def per_device(q, k, v, tissue, dilation_levels, segment_levels, output_matrix):
        dr, dc, width = q.shape
        tiles = dr * dc
        sel = tiles // DILATION_MIN
        groups = HEAD_COUNT // HEADS_TOGETHER
        stacked = HEADS_TOGETHER * tiles
        any_space = pl.BlockSpec(memory_space=pl.ANY)
        vmem = pl.BlockSpec(memory_space=pltpu.VMEM)
        smem = pl.BlockSpec(memory_space=pltpu.SMEM)
        out = pl.pallas_call(
            functools.partial(kernel, n_row, n_col, dr, dc),
            out_shape=jax.ShapeDtypeStruct((tiles, width), BF16),
            in_specs=[any_space, any_space, any_space, vmem, smem, smem],
            out_specs=vmem,
            scratch_shapes=[
                pltpu.VMEM((tiles, width), BF16),
                pltpu.VMEM((2, tiles, width), BF16),
                pltpu.VMEM((2, 3 * tiles, width), BF16),
                pltpu.VMEM((2, 2 * tiles + sel * n_col, width), BF16),
                pltpu.VMEM((2, tiles, width), BF16),
                pltpu.VMEM((2, sel, width), BF16),
                pltpu.VMEM((tiles, tiles), F32),
                pltpu.VMEM((tiles, 3 * tiles), F32),
                pltpu.VMEM((HEAD_COUNT, tiles, 2 * tiles + sel * n_col), F32),
                pltpu.VMEM((groups, stacked, 256), F32),
                pltpu.VMEM((groups, stacked, 1), F32),
                pltpu.VMEM((groups, stacked, 1), F32),
                pltpu.SemaphoreType.DMA((3,)),
                pltpu.SemaphoreType.DMA((8,)),
                pltpu.SemaphoreType.DMA((8,)),
                pltpu.SemaphoreType.DMA((n_col,)),
                pltpu.SemaphoreType.DMA((n_col,)),
            ],
            compiler_params=pltpu.CompilerParams(
                collective_id=0, has_side_effects=True, vmem_limit_bytes=40 * 1024 * 1024
            ),
        )(
            q.reshape(tiles, width), k.reshape(tiles, width), v.reshape(tiles, width),
            tissue, dilation_levels, segment_levels,
        )
        encoded = jnp.dot(out, output_matrix, preferred_element_type=F32).astype(BF16)
        return encoded.reshape(dr, dc, width)

    split = P("row", "col", None)
    return jax.shard_map(
        per_device,
        mesh=mesh,
        in_specs=(split, split, split, P(), P(), P(), P()),
        out_specs=split,
        check_vma=False,
    )
```

```python
import functools
import math

import jax
import jax.numpy as jnp
from jax import lax
from jax.experimental import pallas as pl
from jax.experimental.pallas import tpu as pltpu
from jax.sharding import PartitionSpec as P

HEAD_COUNT = 16
R = 8
DILATION_MIN = 8
NEG_FILL = -1e30
MESH = pl.DeviceIdType.MESH
HEADS_TOGETHER = 4
F32 = jnp.float32
BF16 = jnp.bfloat16


def iota(shape, dim):
    return lax.broadcasted_iota(jnp.int32, shape, dim)


def one_hot(condition):
    return jnp.where(condition, 1.0, 0.0).astype(BF16)


def lane_window(group, head_dimension):
    first = group * HEADS_TOGETHER * head_dimension
    return first // 128 * 128, first % 128


def head_mask(group, head, head_dimension):
    _, offset = lane_window(group, head_dimension)
    lane = iota((1, 256), 1) - offset - head * head_dimension
    return (lane >= 0) & (lane < head_dimension)


def gathered_tissue(tissue, n, key_row, key_col, lanes):
    rows, cols = tissue.shape
    pick = one_hot(iota((n, cols), 1) == key_col(iota((n, cols), 0)))
    by_col = lax.dot_general(
        pick, tissue, (((1,), (1,)), ((), ())), preferred_element_type=F32
    )
    keep = iota((n, rows), 1) == key_row(iota((n, rows), 0))
    kept = jnp.where(keep, by_col, 0.0).astype(BF16)
    return jnp.dot(kept, jnp.ones((rows, lanes), BF16), preferred_element_type=F32)


def window_bias(tissue, n, key_row, key_col, row_offset, column_offset, dr, dc):
    present = gathered_tissue(
        tissue, n, lambda k: key_row(k) + row_offset, lambda k: key_col(k) + column_offset,
        dr * dc,
    )
    k, q = iota((n, dr * dc), 0), iota((n, dr * dc), 1)
    row_gap = jnp.abs(key_row(k) - q // dc)
    col_gap = jnp.abs(key_col(k) - q % dc)
    near = (row_gap <= R) & (col_gap <= R) & (present > 0.5)
    self_key = (row_gap + col_gap) == 0
    return jnp.where(near | self_key, 0.0, NEG_FILL)


def kernel(
    n_row, n_col, dr, dc,
    q_hbm, k_hbm, v_hbm, tissue_ref, dil_ref, seg_ref, out_ref,
    q_ref, query, own_kv, mid_kv, far_kv, halves, chosen, bias_own, bias_mid, bias_far,
    numer, highest, total, local_sem, send_sem, recv_sem, dil_send, dil_recv,
):
    row, col = lax.axis_index("row"), lax.axis_index("col")
    tiles, width = q_ref.shape
    hd = width // HEAD_COUNT
    half = tiles // 2
    corners = 4 * half
    sel = tiles // DILATION_MIN

    loads = [
        pltpu.make_async_copy(k_hbm, own_kv.at[0], local_sem.at[0]),
        pltpu.make_async_copy(v_hbm, own_kv.at[1], local_sem.at[1]),
        pltpu.make_async_copy(q_hbm, q_ref, local_sem.at[2]),
    ]
    for load in loads:
        load.start()

    has_up, has_down = row > 0, row < n_row - 1
    has_left, has_right = col > 0, col < n_col - 1
    up = (lax.rem(row + n_row - 1, n_row), col)
    down = (lax.rem(row + 1, n_row), col)
    left = (row, lax.rem(col + n_col - 1, n_col))
    right = (row, lax.rem(col + 1, n_col))

    barrier = pltpu.get_barrier_semaphore()

    @pl.when(has_up)
    def _():
        pl.semaphore_signal(barrier, inc=1, device_id=up, device_id_type=MESH)

    @pl.when(has_down)
    def _():
        pl.semaphore_signal(barrier, inc=1, device_id=down, device_id_type=MESH)

    for d in range(1, n_col):
        peer = (row, lax.rem(col + d, n_col))
        pl.semaphore_signal(barrier, inc=1, device_id=peer, device_id_type=MESH)

    def remote(src, dst, kind, device):
        return pltpu.make_async_remote_copy(
            src_ref=src, dst_ref=dst, send_sem=send_sem.at[kind], recv_sem=recv_sem.at[kind],
            device_id=device, device_id_type=MESH,
        )

    def mid(first, count):
        return mid_kv.at[:, pl.ds(first, count)]

    def corner(index):
        return far_kv.at[:, pl.ds(index * half, half)]

    left_here, right_here = mid(2 * tiles, half), mid(2 * tiles + half, half)
    to_up = remote(own_kv, mid(tiles, tiles), 0, up)
    to_down = remote(own_kv, mid(0, tiles), 1, down)
    to_left = remote(halves.at[:, pl.ds(0, half)], right_here, 2, left)
    to_right = remote(halves.at[:, pl.ds(half, half)], left_here, 3, right)
    left_to_up = remote(left_here, corner(2), 4, up)
    left_to_down = remote(left_here, corner(0), 5, down)
    right_to_up = remote(right_here, corner(3), 6, up)
    right_to_down = remote(right_here, corner(1), 7, down)

    i, j = iota((tiles, tiles), 0), iota((tiles, tiles), 1)
    within = i % half
    split_order = one_hot(j == within // R * dc + (i // half) * R + within % R)
    local_sel = dc // DILATION_MIN
    s = i % sel
    phase_order = one_hot(j == s // local_sel * dc + s % local_sel * DILATION_MIN + i // sel)
    lane_phase = iota((1, width), 1) // hd % DILATION_MIN
    slot = pl.ds(pl.multiple_of(corners + col * sel, sel), sel)

    loads[0].wait()
    loads[1].wait()
    for t in range(2):
        halves[t] = jnp.dot(split_order, own_kv[t], preferred_element_type=F32).astype(BF16)
    pl.semaphore_wait(
        barrier,
        (n_col - 1) + jnp.where(has_up, 1, 0) + jnp.where(has_down, 1, 0),
    )
    pl.when(has_left)(to_left.start)
    pl.when(has_right)(to_right.start)
    pl.when(has_up)(to_up.start)
    pl.when(has_down)(to_down.start)
    for t in range(2):
        by_phase = jnp.dot(phase_order, own_kv[t], preferred_element_type=F32)
        picked = jnp.zeros((sel, width), F32)
        for p in range(DILATION_MIN):
            picked += jnp.where(lane_phase == p, by_phase[p * sel:(p + 1) * sel], 0.0)
        picked = picked.astype(BF16)
        chosen[t] = picked
        far_kv[t, slot] = picked
    dil = []
    for d in range(1, n_col):
        copy = pltpu.make_async_remote_copy(
            src_ref=chosen, dst_ref=far_kv.at[:, slot],
            send_sem=dil_send.at[d], recv_sem=dil_recv.at[d],
            device_id=(row, lax.rem(col + d, n_col)), device_id_type=MESH,
        )
        copy.start()
        dil.append(copy)

    def clear(ref, first, count):
        ref[:, pl.ds(first, count)] = jnp.zeros((2, count, width), BF16)

    for ref, first, count, have in (
        (mid_kv, 0, tiles, has_up),
        (mid_kv, tiles, tiles, has_down),
        (mid_kv, 2 * tiles, half, has_left),
        (mid_kv, 2 * tiles + half, half, has_right),
        (far_kv, 0, half, has_up & has_left),
        (far_kv, half, half, has_up & has_right),
        (far_kv, 2 * half, half, has_down & has_left),
        (far_kv, 3 * half, half, has_down & has_right),
    ):
        pl.when(jnp.logical_not(have))(functools.partial(clear, ref, first, count))

    tissue = tissue_ref[...].astype(F32).astype(BF16)
    row_offset, column_offset = row * dr, col * dc

    def bias(n, key_row, key_col):
        return window_bias(tissue, n, key_row, key_col, row_offset, column_offset, dr, dc)

    def half_col(k):
        return jnp.where(k % tiles >= half, dc, -R) + k % R

    bias_own[...] = bias(tiles, lambda k: k // dc, lambda k: k % dc)
    for block, shift in ((0, -dr), (1, dr)):
        bias_mid[pl.ds(block * tiles, tiles)] = bias(
            tiles, lambda k: k // dc + shift, lambda k: k % dc
        )
    bias_mid[pl.ds(2 * tiles, tiles)] = bias(tiles, lambda k: k % half // R, half_col)

    factor = math.log2(math.e) / math.sqrt(hd)
    groups = HEAD_COUNT // HEADS_TOGETHER
    loads[2].wait()
    for g in range(groups):
        base, _ = lane_window(g, hd)
        lanes = q_ref[:, pl.ds(base, 256)]
        for h in range(HEADS_TOGETHER):
            query[g, pl.ds(h * tiles, tiles)] = jnp.where(
                head_mask(g, h, hd), lanes, jnp.zeros_like(lanes)
            )

    def attend(kv, extra, first, last):
        values = kv[1].T
        finished = []
        for g in range(groups):
            base, _ = lane_window(g, hd)
            scores = lax.dot_general(
                kv[0, :, pl.ds(base, 256)], query[g], (((1,), (1,)), ((), ())),
                preferred_element_type=F32,
            )
            for h in range(HEADS_TOGETHER):
                head = g * HEADS_TOGETHER + h
                part = scores[:, h * tiles:(h + 1) * tiles] + extra(head)
                top = jnp.max(part, axis=0, keepdims=True)
                if not first:
                    old_top = highest[head]
                    top = jnp.maximum(top, old_top)
                probs = jnp.exp2((part - top) * factor)
                new_total = jnp.sum(probs, axis=0, keepdims=True)
                new_numer = jnp.dot(
                    values[head * hd:(head + 1) * hd], probs.astype(BF16),
                    preferred_element_type=F32,
                )
                if not first:
                    keep = jnp.exp2((old_top - top) * factor)
                    new_total += keep * total[head]
                    new_numer += keep * numer[head]
                if last:
                    finished.append(new_numer * (1.0 / new_total))
                else:
                    highest[head], total[head], numer[head] = top, new_total, new_numer
        return finished

    attend(own_kv, lambda head: bias_own[...], True, False)

    @pl.when(has_left)
    def _():
        to_right.wait_recv()
        pl.when(has_up)(left_to_up.start)
        pl.when(has_down)(left_to_down.start)

    @pl.when(has_right)
    def _():
        to_left.wait_recv()
        pl.when(has_up)(right_to_up.start)
        pl.when(has_down)(right_to_down.start)

    for block, shift in ((0, -dr), (1, dr)):
        shared = bias(tiles, lambda k: k % half // R + shift, half_col)
        for h in range(HEAD_COUNT):
            bias_far[h, pl.ds(block * tiles, tiles)] = shared
    n_dil = sel * n_col

    def dil_row(k):
        return k % sel // local_sel

    def dil_col(k):
        return k // sel * dc + k % local_sel * DILATION_MIN

    k, q = iota((n_dil, tiles), 0), iota((n_dil, tiles), 1)
    same_row = dil_row(k) == q // dc
    for p in range(DILATION_MIN):
        present = gathered_tissue(
            tissue, n_dil, lambda k: dil_row(k) + row_offset, lambda k: dil_col(k) + p, tiles
        )
        allowed = same_row & (present > 0.5)
        key_col = dil_col(k) + p
        apart = key_col ^ (column_offset + q % dc)
        for head in range(p, HEAD_COUNT, DILATION_MIN):
            stride = jnp.left_shift(jnp.int32(DILATION_MIN), dil_ref[head])
            segment = jnp.right_shift(jnp.int32(dc * n_col), seg_ref[head])
            phase_ok = ((key_col ^ head) & (stride - 1)) == 0
            ok = allowed & phase_ok & (apart < segment)
            bias_far[head, pl.ds(corners, n_dil)] = jnp.where(ok, 0.0, NEG_FILL)

    pl.when(has_down)(to_up.wait_recv)
    pl.when(has_up)(to_down.wait_recv)
    attend(mid_kv, lambda head: bias_mid[...], False, False)

    for copy in dil:
        copy.wait_recv()

    @pl.when(has_left)
    def _():
        pl.when(has_up)(left_to_down.wait_recv)
        pl.when(has_down)(left_to_up.wait_recv)

    @pl.when(has_right)
    def _():
        pl.when(has_up)(right_to_down.wait_recv)
        pl.when(has_down)(right_to_up.wait_recv)

    finished = attend(far_kv, lambda head: bias_far[head], False, True)
    out_ref[...] = jnp.concatenate(finished, axis=0).T.astype(BF16)

    pl.when(has_left)(to_left.wait_send)
    pl.when(has_right)(to_right.wait_send)
    pl.when(has_up)(to_up.wait_send)
    pl.when(has_down)(to_down.wait_send)
    pl.when(has_left & has_up)(left_to_up.wait_send)
    pl.when(has_left & has_down)(left_to_down.wait_send)
    pl.when(has_right & has_up)(right_to_up.wait_send)
    pl.when(has_right & has_down)(right_to_down.wait_send)
    for copy in dil:
        copy.wait_send()


def solution(mesh):
    n_row, n_col = mesh.shape["row"], mesh.shape["col"]

    def per_device(q, k, v, tissue, dilation_levels, segment_levels, output_matrix):
        dr, dc, width = q.shape
        tiles = dr * dc
        sel = tiles // DILATION_MIN
        groups = HEAD_COUNT // HEADS_TOGETHER
        any_space = pl.BlockSpec(memory_space=pl.ANY)
        vmem = pl.BlockSpec(memory_space=pltpu.VMEM)
        smem = pl.BlockSpec(memory_space=pltpu.SMEM)
        out = pl.pallas_call(
            functools.partial(kernel, n_row, n_col, dr, dc),
            out_shape=jax.ShapeDtypeStruct((tiles, width), BF16),
            in_specs=[any_space, any_space, any_space, vmem, smem, smem],
            out_specs=vmem,
            scratch_shapes=[
                pltpu.VMEM((tiles, width), BF16),
                pltpu.VMEM((groups, HEADS_TOGETHER * tiles, 256), BF16),
                pltpu.VMEM((2, tiles, width), BF16),
                pltpu.VMEM((2, 3 * tiles, width), BF16),
                pltpu.VMEM((2, 2 * tiles + sel * n_col, width), BF16),
                pltpu.VMEM((2, tiles, width), BF16),
                pltpu.VMEM((2, sel, width), BF16),
                pltpu.VMEM((tiles, tiles), F32),
                pltpu.VMEM((3 * tiles, tiles), F32),
                pltpu.VMEM((HEAD_COUNT, 2 * tiles + sel * n_col, tiles), F32),
                pltpu.VMEM((HEAD_COUNT, width // HEAD_COUNT, tiles), F32),
                pltpu.VMEM((HEAD_COUNT, 1, tiles), F32),
                pltpu.VMEM((HEAD_COUNT, 1, tiles), F32),
                pltpu.SemaphoreType.DMA((3,)),
                pltpu.SemaphoreType.DMA((8,)),
                pltpu.SemaphoreType.DMA((8,)),
                pltpu.SemaphoreType.DMA((n_col,)),
                pltpu.SemaphoreType.DMA((n_col,)),
            ],
            compiler_params=pltpu.CompilerParams(
                collective_id=0, has_side_effects=True, vmem_limit_bytes=56 * 1024 * 1024
            ),
        )(
            q.reshape(tiles, width), k.reshape(tiles, width), v.reshape(tiles, width),
            tissue, dilation_levels, segment_levels,
        )
        encoded = jnp.dot(out, output_matrix, preferred_element_type=F32).astype(BF16)
        return encoded.reshape(dr, dc, width)

    split = P("row", "col", None)
    return jax.shard_map(
        per_device,
        mesh=mesh,
        in_specs=(split, split, split, P(), P(), P(), P()),
        out_specs=split,
        check_vma=False,
    )
```

```python
import functools
import math

import jax
import jax.numpy as jnp
from jax import lax
from jax.experimental import pallas as pl
from jax.experimental.pallas import tpu as pltpu
from jax.sharding import PartitionSpec as P

HEAD_COUNT = 16
R = 8
DILATION_MIN = 8
NEG_FILL = -1e30
MESH = pl.DeviceIdType.MESH
HEADS_TOGETHER = 4
F32 = jnp.float32
BF16 = jnp.bfloat16


def iota(shape, dim):
    return lax.broadcasted_iota(jnp.int32, shape, dim)


def one_hot(condition):
    return jnp.where(condition, 1.0, 0.0).astype(BF16)


def lane_window(group, head_dimension):
    first = group * HEADS_TOGETHER * head_dimension
    return first // 128 * 128, first % 128


def head_mask(group, head, head_dimension):
    _, offset = lane_window(group, head_dimension)
    lane = iota((1, 256), 1) - offset - head * head_dimension
    return (lane >= 0) & (lane < head_dimension)


def gathered_tissue(tissue, n, key_row, key_col, lanes):
    rows, cols = tissue.shape
    pick = one_hot(iota((n, cols), 1) == key_col(iota((n, cols), 0)))
    by_col = lax.dot_general(
        pick, tissue, (((1,), (1,)), ((), ())), preferred_element_type=F32
    )
    keep = iota((n, rows), 1) == key_row(iota((n, rows), 0))
    kept = jnp.where(keep, by_col, 0.0).astype(BF16)
    return jnp.dot(kept, jnp.ones((rows, lanes), BF16), preferred_element_type=F32)


def window_bias(tissue, n, key_row, key_col, row_offset, column_offset, dr, dc):
    present = gathered_tissue(
        tissue, n, lambda k: key_row(k) + row_offset, lambda k: key_col(k) + column_offset,
        dr * dc,
    )
    k, q = iota((n, dr * dc), 0), iota((n, dr * dc), 1)
    row_gap = jnp.abs(key_row(k) - q // dc)
    col_gap = jnp.abs(key_col(k) - q % dc)
    near = (row_gap <= R) & (col_gap <= R) & (present > 0.5)
    self_key = (row_gap + col_gap) == 0
    return jnp.where(near | self_key, 0.0, NEG_FILL)


def kernel(
    n_row, n_col, dr, dc,
    q_hbm, k_hbm, v_hbm, tissue_ref, dil_ref, seg_ref, out_ref,
    q_ref, query, own_kv, mid_kv, far_kv, halves, chosen, bias_own, bias_mid, bias_far,
    numer, highest, total, local_sem, send_sem, recv_sem, dil_send, dil_recv,
):
    row, col = lax.axis_index("row"), lax.axis_index("col")
    tiles, width = q_ref.shape
    hd = width // HEAD_COUNT
    half = tiles // 2
    corners = 4 * half
    sel = tiles // DILATION_MIN

    loads = [
        pltpu.make_async_copy(k_hbm, own_kv.at[0], local_sem.at[0]),
        pltpu.make_async_copy(v_hbm, own_kv.at[1], local_sem.at[1]),
        pltpu.make_async_copy(q_hbm, q_ref, local_sem.at[2]),
    ]
    for load in loads:
        load.start()

    has_up, has_down = row > 0, row < n_row - 1
    has_left, has_right = col > 0, col < n_col - 1
    up = (lax.rem(row + n_row - 1, n_row), col)
    down = (lax.rem(row + 1, n_row), col)
    left = (row, lax.rem(col + n_col - 1, n_col))
    right = (row, lax.rem(col + 1, n_col))

    barrier = pltpu.get_barrier_semaphore()

    @pl.when(has_up)
    def _():
        pl.semaphore_signal(barrier, inc=1, device_id=up, device_id_type=MESH)

    @pl.when(has_down)
    def _():
        pl.semaphore_signal(barrier, inc=1, device_id=down, device_id_type=MESH)

    @pl.when(has_left)
    def _():
        pl.semaphore_signal(barrier, inc=1, device_id=left, device_id_type=MESH)

    @pl.when(has_right)
    def _():
        pl.semaphore_signal(barrier, inc=1, device_id=right, device_id_type=MESH)

    partner = (row, col + 1 - 2 * (col % 2))
    same_parity = [(row, lax.rem(col + 2 * d, n_col)) for d in range(1, n_col // 2)]
    for peer in same_parity:
        pl.semaphore_signal(barrier, inc=1, device_id=peer, device_id_type=MESH)

    def remote(src, dst, kind, device):
        return pltpu.make_async_remote_copy(
            src_ref=src, dst_ref=dst, send_sem=send_sem.at[kind], recv_sem=recv_sem.at[kind],
            device_id=device, device_id_type=MESH,
        )

    def mid(first, count):
        return mid_kv.at[:, pl.ds(first, count)]

    to_up = remote(own_kv, mid(tiles, tiles), 0, up)
    to_down = remote(own_kv, mid(0, tiles), 1, down)
    to_left, to_right, left_to_up, left_to_down, right_to_up, right_to_down = (
        [], [], [], [], [], []
    )
    for t in range(2):
        left_here = mid_kv.at[t, pl.ds(2 * tiles, half)]
        right_here = mid_kv.at[t, pl.ds(2 * tiles + half, half)]
        corner = [far_kv.at[t, pl.ds(index * half, half)] for index in range(4)]
        sem = 2 + 6 * t
        to_left.append(remote(halves.at[t, pl.ds(0, half)], right_here, sem, left))
        to_right.append(remote(halves.at[t, pl.ds(half, half)], left_here, sem + 1, right))
        left_to_up.append(remote(left_here, corner[2], sem + 2, up))
        left_to_down.append(remote(left_here, corner[0], sem + 3, down))
        right_to_up.append(remote(right_here, corner[3], sem + 4, up))
        right_to_down.append(remote(right_here, corner[1], sem + 5, down))

    i, j = iota((tiles, tiles), 0), iota((tiles, tiles), 1)
    within = i % half
    split_order = one_hot(j == within // R * dc + (i // half) * R + within % R)
    local_sel = dc // DILATION_MIN
    s = i % sel
    phase_order = one_hot(j == s // local_sel * dc + s % local_sel * DILATION_MIN + i // sel)
    lane_phase = iota((1, width), 1) // hd % DILATION_MIN
    pairs = n_col // 2
    own_slot = col % 2 * pairs + col // 2
    slot = pl.ds(pl.multiple_of(corners + own_slot * sel, sel), sel)
    parity_slots = pl.ds(pl.multiple_of(corners + col % 2 * pairs * sel, sel), pairs * sel)

    loads[0].wait()
    loads[1].wait()
    for t in range(2):
        halves[t] = jnp.dot(split_order, own_kv[t], preferred_element_type=F32).astype(BF16)
    pl.semaphore_wait(
        barrier,
        len(same_parity)
        + jnp.where(has_up, 1, 0) + jnp.where(has_down, 1, 0)
        + jnp.where(has_left, 1, 0) + jnp.where(has_right, 1, 0),
    )
    for t in range(2):
        pl.when(has_left)(to_left[t].start)
        pl.when(has_right)(to_right[t].start)
    pl.when(has_up)(to_up.start)
    pl.when(has_down)(to_down.start)
    for t in range(2):
        by_phase = jnp.dot(phase_order, own_kv[t], preferred_element_type=F32)
        picked = jnp.zeros((sel, width), F32)
        for p in range(DILATION_MIN):
            picked += jnp.where(lane_phase == p, by_phase[p * sel:(p + 1) * sel], 0.0)
        picked = picked.astype(BF16)
        chosen[t] = picked
        far_kv[t, slot] = picked
    dil = []
    for d, peer in enumerate(same_parity):
        copy = pltpu.make_async_remote_copy(
            src_ref=chosen, dst_ref=far_kv.at[:, slot],
            send_sem=dil_send.at[d], recv_sem=dil_recv.at[d],
            device_id=peer, device_id_type=MESH,
        )
        copy.start()
        dil.append(copy)
    to_partner = pltpu.make_async_remote_copy(
        src_ref=far_kv.at[:, parity_slots], dst_ref=far_kv.at[:, parity_slots],
        send_sem=dil_send.at[pairs], recv_sem=dil_recv.at[pairs],
        device_id=partner, device_id_type=MESH,
    )

    def clear(ref, first, count):
        ref[:, pl.ds(first, count)] = jnp.zeros((2, count, width), BF16)

    for ref, first, count, have in (
        (mid_kv, 0, tiles, has_up),
        (mid_kv, tiles, tiles, has_down),
        (mid_kv, 2 * tiles, half, has_left),
        (mid_kv, 2 * tiles + half, half, has_right),
        (far_kv, 0, half, has_up & has_left),
        (far_kv, half, half, has_up & has_right),
        (far_kv, 2 * half, half, has_down & has_left),
        (far_kv, 3 * half, half, has_down & has_right),
    ):
        pl.when(jnp.logical_not(have))(functools.partial(clear, ref, first, count))

    tissue = tissue_ref[...].astype(F32).astype(BF16)
    row_offset, column_offset = row * dr, col * dc

    def bias(n, key_row, key_col):
        return window_bias(tissue, n, key_row, key_col, row_offset, column_offset, dr, dc)

    def half_col(k):
        return jnp.where(k % tiles >= half, dc, -R) + k % R

    bias_own[...] = bias(tiles, lambda k: k // dc, lambda k: k % dc)
    for block, shift in ((0, -dr), (1, dr)):
        bias_mid[pl.ds(block * tiles, tiles)] = bias(
            tiles, lambda k: k // dc + shift, lambda k: k % dc
        )
    bias_mid[pl.ds(2 * tiles, tiles)] = bias(tiles, lambda k: k % half // R, half_col)

    factor = math.log2(math.e) / math.sqrt(hd)
    groups = HEAD_COUNT // HEADS_TOGETHER
    loads[2].wait()
    for g in range(groups):
        base, _ = lane_window(g, hd)
        lanes = q_ref[:, pl.ds(base, 256)]
        for h in range(HEADS_TOGETHER):
            query[g, pl.ds(h * tiles, tiles)] = jnp.where(
                head_mask(g, h, hd), lanes, jnp.zeros_like(lanes)
            )

    def attend(kv, extra, first, last):
        values = kv[1].T
        finished = []
        for g in range(groups):
            base, _ = lane_window(g, hd)
            scores = lax.dot_general(
                kv[0, :, pl.ds(base, 256)], query[g], (((1,), (1,)), ((), ())),
                preferred_element_type=F32,
            )
            for h in range(HEADS_TOGETHER):
                head = g * HEADS_TOGETHER + h
                part = scores[:, h * tiles:(h + 1) * tiles] + extra(head)
                top = jnp.max(part, axis=0, keepdims=True)
                if not first:
                    old_top = highest[head]
                    top = jnp.maximum(top, old_top)
                probs = jnp.exp2((part - top) * factor)
                new_total = jnp.sum(probs, axis=0, keepdims=True)
                new_numer = jnp.dot(
                    values[head * hd:(head + 1) * hd], probs.astype(BF16),
                    preferred_element_type=F32,
                )
                if not first:
                    keep = jnp.exp2((old_top - top) * factor)
                    new_total += keep * total[head]
                    new_numer += keep * numer[head]
                if last:
                    finished.append(new_numer * (1.0 / new_total))
                else:
                    highest[head], total[head], numer[head] = top, new_total, new_numer
        return finished

    attend(own_kv, lambda head: bias_own[...], True, False)

    for t in range(2):

        @pl.when(has_left)
        def _(t=t):
            to_right[t].wait_recv()
            pl.when(has_up)(left_to_up[t].start)
            pl.when(has_down)(left_to_down[t].start)

        @pl.when(has_right)
        def _(t=t):
            to_left[t].wait_recv()
            pl.when(has_up)(right_to_up[t].start)
            pl.when(has_down)(right_to_down[t].start)

    for copy in dil:
        copy.wait_recv()
    to_partner.start()

    for block, shift in ((0, -dr), (1, dr)):
        shared = bias(tiles, lambda k: k % half // R + shift, half_col)
        for h in range(HEAD_COUNT):
            bias_far[h, pl.ds(block * tiles, tiles)] = shared
    n_dil = sel * n_col

    def dil_row(k):
        return k % sel // local_sel

    def dil_col(k):
        place = k // sel
        device = place % pairs * 2 + place // pairs
        return device * dc + k % local_sel * DILATION_MIN

    k, q = iota((n_dil, tiles), 0), iota((n_dil, tiles), 1)
    same_row = dil_row(k) == q // dc
    for p in range(DILATION_MIN):
        present = gathered_tissue(
            tissue, n_dil, lambda k: dil_row(k) + row_offset, lambda k: dil_col(k) + p, tiles
        )
        allowed = same_row & (present > 0.5)
        key_col = dil_col(k) + p
        apart = key_col ^ (column_offset + q % dc)
        for head in range(p, HEAD_COUNT, DILATION_MIN):
            stride = jnp.left_shift(jnp.int32(DILATION_MIN), dil_ref[head])
            segment = jnp.right_shift(jnp.int32(dc * n_col), seg_ref[head])
            phase_ok = ((key_col ^ head) & (stride - 1)) == 0
            ok = allowed & phase_ok & (apart < segment)
            bias_far[head, pl.ds(corners, n_dil)] = jnp.where(ok, 0.0, NEG_FILL)

    pl.when(has_down)(to_up.wait_recv)
    pl.when(has_up)(to_down.wait_recv)
    attend(mid_kv, lambda head: bias_mid[...], False, False)

    to_partner.wait_recv()
    for t in range(2):
        pl.when(has_left & has_up)(left_to_down[t].wait_recv)
        pl.when(has_left & has_down)(left_to_up[t].wait_recv)
        pl.when(has_right & has_up)(right_to_down[t].wait_recv)
        pl.when(has_right & has_down)(right_to_up[t].wait_recv)

    finished = attend(far_kv, lambda head: bias_far[head], False, True)
    out_ref[...] = jnp.concatenate(finished, axis=0).T.astype(BF16)

    pl.when(has_up)(to_up.wait_send)
    pl.when(has_down)(to_down.wait_send)
    for t in range(2):
        pl.when(has_left)(to_left[t].wait_send)
        pl.when(has_right)(to_right[t].wait_send)
        pl.when(has_left & has_up)(left_to_up[t].wait_send)
        pl.when(has_left & has_down)(left_to_down[t].wait_send)
        pl.when(has_right & has_up)(right_to_up[t].wait_send)
        pl.when(has_right & has_down)(right_to_down[t].wait_send)
    for copy in dil:
        copy.wait_send()
    to_partner.wait_send()


def solution(mesh):
    n_row, n_col = mesh.shape["row"], mesh.shape["col"]

    def per_device(q, k, v, tissue, dilation_levels, segment_levels, output_matrix):
        dr, dc, width = q.shape
        tiles = dr * dc
        sel = tiles // DILATION_MIN
        groups = HEAD_COUNT // HEADS_TOGETHER
        hbm = pl.BlockSpec(memory_space=pltpu.HBM)
        vmem = pl.BlockSpec(memory_space=pltpu.VMEM)
        smem = pl.BlockSpec(memory_space=pltpu.SMEM)
        out = pl.pallas_call(
            functools.partial(kernel, n_row, n_col, dr, dc),
            out_shape=jax.ShapeDtypeStruct((tiles, width), BF16),
            in_specs=[hbm, hbm, hbm, vmem, smem, smem],
            out_specs=vmem,
            scratch_shapes=[
                pltpu.VMEM((tiles, width), BF16),
                pltpu.VMEM((groups, HEADS_TOGETHER * tiles, 256), BF16),
                pltpu.VMEM((2, tiles, width), BF16),
                pltpu.VMEM((2, 3 * tiles, width), BF16),
                pltpu.VMEM((2, 2 * tiles + sel * n_col, width), BF16),
                pltpu.VMEM((2, tiles, width), BF16),
                pltpu.VMEM((2, sel, width), BF16),
                pltpu.VMEM((tiles, tiles), F32),
                pltpu.VMEM((3 * tiles, tiles), F32),
                pltpu.VMEM((HEAD_COUNT, 2 * tiles + sel * n_col, tiles), F32),
                pltpu.VMEM((HEAD_COUNT, width // HEAD_COUNT, tiles), F32),
                pltpu.VMEM((HEAD_COUNT, 1, tiles), F32),
                pltpu.VMEM((HEAD_COUNT, 1, tiles), F32),
                pltpu.SemaphoreType.DMA((3,)),
                pltpu.SemaphoreType.DMA((14,)),
                pltpu.SemaphoreType.DMA((14,)),
                pltpu.SemaphoreType.DMA((n_col,)),
                pltpu.SemaphoreType.DMA((n_col,)),
            ],
            compiler_params=pltpu.CompilerParams(
                collective_id=0, has_side_effects=True, vmem_limit_bytes=56 * 1024 * 1024
            ),
        )(
            q.reshape(tiles, width), k.reshape(tiles, width), v.reshape(tiles, width),
            tissue, dilation_levels, segment_levels,
        )
        encoded = jnp.dot(out, output_matrix, preferred_element_type=F32).astype(BF16)
        return encoded.reshape(dr, dc, width)

    split = P("row", "col", None)
    return jax.shard_map(
        per_device,
        mesh=mesh,
        in_specs=(split, split, split, P(), P(), P(), P()),
        out_specs=split,
        check_vma=False,
    )
```

```python
import functools
import math

import jax
import jax.numpy as jnp
from jax import lax
from jax.experimental import pallas as pl
from jax.experimental.pallas import tpu as pltpu
from jax.sharding import PartitionSpec as P

HEAD_COUNT = 16
R = 8
DILATION_MIN = 8
NEG_FILL = -1e30
MESH = pl.DeviceIdType.MESH
HEADS_TOGETHER = 4
F32 = jnp.float32
BF16 = jnp.bfloat16


def iota(shape, dim):
    return lax.broadcasted_iota(jnp.int32, shape, dim)


def one_hot(condition):
    return jnp.where(condition, 1.0, 0.0).astype(BF16)


def lane_window(group, head_dimension):
    first = group * HEADS_TOGETHER * head_dimension
    return first // 128 * 128, first % 128


def head_mask(group, head, head_dimension):
    _, offset = lane_window(group, head_dimension)
    lane = iota((1, 256), 1) - offset - head * head_dimension
    return (lane >= 0) & (lane < head_dimension)


def gathered_tissue(tissue, n, key_row, key_col, lanes):
    rows, cols = tissue.shape
    pick = one_hot(iota((n, cols), 1) == key_col(iota((n, cols), 0)))
    by_col = lax.dot_general(
        pick, tissue, (((1,), (1,)), ((), ())), preferred_element_type=F32
    )
    keep = iota((n, rows), 1) == key_row(iota((n, rows), 0))
    kept = jnp.where(keep, by_col, 0.0).astype(BF16)
    return jnp.dot(kept, jnp.ones((rows, lanes), BF16), preferred_element_type=F32)


def window_bias(tissue, n, key_row, key_col, row_offset, column_offset, dr, dc):
    present = gathered_tissue(
        tissue, n, lambda k: key_row(k) + row_offset, lambda k: key_col(k) + column_offset,
        dr * dc,
    )
    k, q = iota((n, dr * dc), 0), iota((n, dr * dc), 1)
    row_gap = jnp.abs(key_row(k) - q // dc)
    col_gap = jnp.abs(key_col(k) - q % dc)
    near = (row_gap <= R) & (col_gap <= R) & (present > 0.5)
    self_key = (row_gap + col_gap) == 0
    return jnp.where(near | self_key, 0.0, NEG_FILL)


def kernel(
    n_row, n_col, dr, dc,
    q_hbm, k_hbm, v_hbm, tissue_ref, dil_ref, seg_ref, out_ref,
    q_ref, query, own_kv, mid_kv, far_kv, halves, chosen, bias_own, bias_mid, bias_far,
    numer, highest, total, local_sem, send_sem, recv_sem, dil_send, dil_recv,
):
    row, col = lax.axis_index("row"), lax.axis_index("col")
    tiles, width = q_ref.shape
    hd = width // HEAD_COUNT
    half = tiles // 2
    corners = 4 * half
    sel = tiles // DILATION_MIN

    loads = [
        pltpu.make_async_copy(k_hbm, own_kv.at[0], local_sem.at[0]),
        pltpu.make_async_copy(v_hbm, own_kv.at[1], local_sem.at[1]),
        pltpu.make_async_copy(q_hbm, q_ref, local_sem.at[2]),
    ]
    for load in loads:
        load.start()

    has_up, has_down = row > 0, row < n_row - 1
    has_left, has_right = col > 0, col < n_col - 1
    up = (lax.rem(row + n_row - 1, n_row), col)
    down = (lax.rem(row + 1, n_row), col)
    left = (row, lax.rem(col + n_col - 1, n_col))
    right = (row, lax.rem(col + 1, n_col))

    barrier = pltpu.get_barrier_semaphore()

    @pl.when(has_up)
    def _():
        pl.semaphore_signal(barrier, inc=1, device_id=up, device_id_type=MESH)

    @pl.when(has_down)
    def _():
        pl.semaphore_signal(barrier, inc=1, device_id=down, device_id_type=MESH)

    @pl.when(has_left)
    def _():
        pl.semaphore_signal(barrier, inc=1, device_id=left, device_id_type=MESH)

    @pl.when(has_right)
    def _():
        pl.semaphore_signal(barrier, inc=1, device_id=right, device_id_type=MESH)

    partner = (row, col + 1 - 2 * (col % 2))
    same_parity = [(row, lax.rem(col + 2 * d, n_col)) for d in range(1, n_col // 2)]
    for peer in same_parity:
        pl.semaphore_signal(barrier, inc=1, device_id=peer, device_id_type=MESH)

    def remote(src, dst, kind, device):
        return pltpu.make_async_remote_copy(
            src_ref=src, dst_ref=dst, send_sem=send_sem.at[kind], recv_sem=recv_sem.at[kind],
            device_id=device, device_id_type=MESH,
        )

    def mid(first, count):
        return mid_kv.at[:, pl.ds(first, count)]

    to_up = remote(own_kv, mid(tiles, tiles), 0, up)
    to_down = remote(own_kv, mid(0, tiles), 1, down)
    to_left, to_right, left_to_up, left_to_down, right_to_up, right_to_down = (
        [], [], [], [], [], []
    )
    for t in range(2):
        left_here = mid_kv.at[t, pl.ds(2 * tiles, half)]
        right_here = mid_kv.at[t, pl.ds(2 * tiles + half, half)]
        corner = [far_kv.at[t, pl.ds(index * half, half)] for index in range(4)]
        sem = 2 + 6 * t
        to_left.append(remote(halves.at[t, pl.ds(0, half)], right_here, sem, left))
        to_right.append(remote(halves.at[t, pl.ds(half, half)], left_here, sem + 1, right))
        left_to_up.append(remote(left_here, corner[2], sem + 2, up))
        left_to_down.append(remote(left_here, corner[0], sem + 3, down))
        right_to_up.append(remote(right_here, corner[3], sem + 4, up))
        right_to_down.append(remote(right_here, corner[1], sem + 5, down))

    i, j = iota((tiles, tiles), 0), iota((tiles, tiles), 1)
    within = i % half
    split_order = one_hot(j == within // R * dc + (i // half) * R + within % R)
    local_sel = dc // DILATION_MIN
    s = i % sel
    phase_order = one_hot(j == s // local_sel * dc + s % local_sel * DILATION_MIN + i // sel)
    lane_phase = iota((1, width), 1) // hd % DILATION_MIN
    pairs = n_col // 2
    own_slot = col % 2 * pairs + col // 2
    slot = pl.ds(pl.multiple_of(corners + own_slot * sel, sel), sel)
    parity_slots = pl.ds(pl.multiple_of(corners + col % 2 * pairs * sel, sel), pairs * sel)

    loads[0].wait()
    loads[1].wait()
    for t in range(2):
        halves[t] = jnp.dot(split_order, own_kv[t], preferred_element_type=F32).astype(BF16)
    pl.semaphore_wait(
        barrier,
        len(same_parity)
        + jnp.where(has_up, 1, 0) + jnp.where(has_down, 1, 0)
        + jnp.where(has_left, 1, 0) + jnp.where(has_right, 1, 0),
    )
    for t in range(2):
        pl.when(has_left)(to_left[t].start)
        pl.when(has_right)(to_right[t].start)
    pl.when(has_up)(to_up.start)
    pl.when(has_down)(to_down.start)
    for t in range(2):
        by_phase = jnp.dot(phase_order, own_kv[t], preferred_element_type=F32)
        picked = jnp.zeros((sel, width), F32)
        for p in range(DILATION_MIN):
            picked += jnp.where(lane_phase == p, by_phase[p * sel:(p + 1) * sel], 0.0)
        picked = picked.astype(BF16)
        chosen[t] = picked
        far_kv[t, slot] = picked
    dil = []
    for d, peer in enumerate(same_parity):
        copy = pltpu.make_async_remote_copy(
            src_ref=chosen, dst_ref=far_kv.at[:, slot],
            send_sem=dil_send.at[d], recv_sem=dil_recv.at[d],
            device_id=peer, device_id_type=MESH,
        )
        copy.start()
        dil.append(copy)
    to_partner = pltpu.make_async_remote_copy(
        src_ref=far_kv.at[:, parity_slots], dst_ref=far_kv.at[:, parity_slots],
        send_sem=dil_send.at[pairs], recv_sem=dil_recv.at[pairs],
        device_id=partner, device_id_type=MESH,
    )

    def clear(ref, first, count):
        ref[:, pl.ds(first, count)] = jnp.zeros((2, count, width), BF16)

    for ref, first, count, have in (
        (mid_kv, 0, tiles, has_up),
        (mid_kv, tiles, tiles, has_down),
        (mid_kv, 2 * tiles, half, has_left),
        (mid_kv, 2 * tiles + half, half, has_right),
        (far_kv, 0, half, has_up & has_left),
        (far_kv, half, half, has_up & has_right),
        (far_kv, 2 * half, half, has_down & has_left),
        (far_kv, 3 * half, half, has_down & has_right),
    ):
        pl.when(jnp.logical_not(have))(functools.partial(clear, ref, first, count))

    tissue = tissue_ref[...].astype(F32).astype(BF16)
    row_offset, column_offset = row * dr, col * dc

    def bias(n, key_row, key_col):
        return window_bias(tissue, n, key_row, key_col, row_offset, column_offset, dr, dc)

    def half_col(k):
        return jnp.where(k % tiles >= half, dc, -R) + k % R

    bias_own[...] = bias(tiles, lambda k: k // dc, lambda k: k % dc)
    for block, shift in ((0, -dr), (1, dr)):
        bias_mid[pl.ds(block * tiles, tiles)] = bias(
            tiles, lambda k: k // dc + shift, lambda k: k % dc
        )
    bias_mid[pl.ds(2 * tiles, tiles)] = bias(tiles, lambda k: k % half // R, half_col)

    factor = math.log2(math.e) / math.sqrt(hd)
    groups = HEAD_COUNT // HEADS_TOGETHER
    loads[2].wait()
    for g in range(groups):
        base, _ = lane_window(g, hd)
        lanes = q_ref[:, pl.ds(base, 256)]
        for h in range(HEADS_TOGETHER):
            query[g, pl.ds(h * tiles, tiles)] = jnp.where(
                head_mask(g, h, hd), lanes, jnp.zeros_like(lanes)
            )

    def attend(kv, begin, count, extra, first, last):
        values = kv[1, pl.ds(begin, count)].T
        finished = []
        for g in range(groups):
            base, _ = lane_window(g, hd)
            scores = lax.dot_general(
                kv[0, pl.ds(begin, count), pl.ds(base, 256)], query[g], (((1,), (1,)), ((), ())),
                preferred_element_type=F32,
            )
            for h in range(HEADS_TOGETHER):
                head = g * HEADS_TOGETHER + h
                part = scores[:, h * tiles:(h + 1) * tiles] + extra(head)
                top = jnp.max(part, axis=0, keepdims=True)
                if not first:
                    old_top = highest[head]
                    top = jnp.maximum(top, old_top)
                probs = jnp.exp2((part - top) * factor)
                new_total = jnp.sum(probs, axis=0, keepdims=True)
                new_numer = jnp.dot(
                    values[head * hd:(head + 1) * hd], probs.astype(BF16),
                    preferred_element_type=F32,
                )
                if not first:
                    keep = jnp.exp2((old_top - top) * factor)
                    new_total += keep * total[head]
                    new_numer += keep * numer[head]
                if last:
                    finished.append(new_numer * (1.0 / new_total))
                else:
                    highest[head], total[head], numer[head] = top, new_total, new_numer
        return finished

    attend(own_kv, 0, tiles, lambda head: bias_own[...], True, False)

    for block, shift in ((0, -dr), (1, dr)):
        shared = bias(tiles, lambda k: k % half // R + shift, half_col)
        for h in range(HEAD_COUNT):
            bias_far[h, pl.ds(block * tiles, tiles)] = shared
    n_dil = sel * n_col

    def dil_row(k):
        return k % sel // local_sel

    def dil_col(k):
        place = k // sel
        device = place % pairs * 2 + place // pairs
        return device * dc + k % local_sel * DILATION_MIN

    k, q = iota((n_dil, tiles), 0), iota((n_dil, tiles), 1)
    same_row = dil_row(k) == q // dc
    for p in range(DILATION_MIN):
        present = gathered_tissue(
            tissue, n_dil, lambda k: dil_row(k) + row_offset, lambda k: dil_col(k) + p, tiles
        )
        allowed = same_row & (present > 0.5)
        key_col = dil_col(k) + p
        apart = key_col ^ (column_offset + q % dc)
        for head in range(p, HEAD_COUNT, DILATION_MIN):
            stride = jnp.left_shift(jnp.int32(DILATION_MIN), dil_ref[head])
            segment = jnp.right_shift(jnp.int32(dc * n_col), seg_ref[head])
            phase_ok = ((key_col ^ head) & (stride - 1)) == 0
            ok = allowed & phase_ok & (apart < segment)
            bias_far[head, pl.ds(corners, n_dil)] = jnp.where(ok, 0.0, NEG_FILL)

    pl.when(has_down)(to_up.wait_recv)
    pl.when(has_up)(to_down.wait_recv)
    attend(mid_kv, 0, 2 * tiles, lambda head: bias_mid[pl.ds(0, 2 * tiles)], False, False)

    for t in range(2):

        @pl.when(has_left)
        def _(t=t):
            to_right[t].wait_recv()
            pl.when(has_up)(left_to_up[t].start)
            pl.when(has_down)(left_to_down[t].start)

        @pl.when(has_right)
        def _(t=t):
            to_left[t].wait_recv()
            pl.when(has_up)(right_to_up[t].start)
            pl.when(has_down)(right_to_down[t].start)

    for copy in dil:
        copy.wait_recv()
    to_partner.start()

    attend(
        mid_kv, 2 * tiles, tiles, lambda head: bias_mid[pl.ds(2 * tiles, tiles)], False, False
    )
    to_partner.wait_recv()
    for t in range(2):
        pl.when(has_left & has_up)(left_to_down[t].wait_recv)
        pl.when(has_left & has_down)(left_to_up[t].wait_recv)
        pl.when(has_right & has_up)(right_to_down[t].wait_recv)
        pl.when(has_right & has_down)(right_to_up[t].wait_recv)

    finished = attend(
        far_kv, 0, corners + n_dil, lambda head: bias_far[head], False, True
    )
    out_ref[...] = jnp.concatenate(finished, axis=0).T.astype(BF16)

    pl.when(has_up)(to_up.wait_send)
    pl.when(has_down)(to_down.wait_send)
    for t in range(2):
        pl.when(has_left)(to_left[t].wait_send)
        pl.when(has_right)(to_right[t].wait_send)
        pl.when(has_left & has_up)(left_to_up[t].wait_send)
        pl.when(has_left & has_down)(left_to_down[t].wait_send)
        pl.when(has_right & has_up)(right_to_up[t].wait_send)
        pl.when(has_right & has_down)(right_to_down[t].wait_send)
    for copy in dil:
        copy.wait_send()
    to_partner.wait_send()


def solution(mesh):
    n_row, n_col = mesh.shape["row"], mesh.shape["col"]

    def per_device(q, k, v, tissue, dilation_levels, segment_levels, output_matrix):
        dr, dc, width = q.shape
        tiles = dr * dc
        sel = tiles // DILATION_MIN
        groups = HEAD_COUNT // HEADS_TOGETHER
        hbm = pl.BlockSpec(memory_space=pltpu.HBM)
        vmem = pl.BlockSpec(memory_space=pltpu.VMEM)
        smem = pl.BlockSpec(memory_space=pltpu.SMEM)
        out = pl.pallas_call(
            functools.partial(kernel, n_row, n_col, dr, dc),
            out_shape=jax.ShapeDtypeStruct((tiles, width), BF16),
            in_specs=[hbm, hbm, hbm, vmem, smem, smem],
            out_specs=vmem,
            scratch_shapes=[
                pltpu.VMEM((tiles, width), BF16),
                pltpu.VMEM((groups, HEADS_TOGETHER * tiles, 256), BF16),
                pltpu.VMEM((2, tiles, width), BF16),
                pltpu.VMEM((2, 3 * tiles, width), BF16),
                pltpu.VMEM((2, 2 * tiles + sel * n_col, width), BF16),
                pltpu.VMEM((2, tiles, width), BF16),
                pltpu.VMEM((2, sel, width), BF16),
                pltpu.VMEM((tiles, tiles), F32),
                pltpu.VMEM((3 * tiles, tiles), F32),
                pltpu.VMEM((HEAD_COUNT, 2 * tiles + sel * n_col, tiles), F32),
                pltpu.VMEM((HEAD_COUNT, width // HEAD_COUNT, tiles), F32),
                pltpu.VMEM((HEAD_COUNT, 1, tiles), F32),
                pltpu.VMEM((HEAD_COUNT, 1, tiles), F32),
                pltpu.SemaphoreType.DMA((3,)),
                pltpu.SemaphoreType.DMA((14,)),
                pltpu.SemaphoreType.DMA((14,)),
                pltpu.SemaphoreType.DMA((n_col,)),
                pltpu.SemaphoreType.DMA((n_col,)),
            ],
            compiler_params=pltpu.CompilerParams(
                collective_id=0, has_side_effects=True, vmem_limit_bytes=56 * 1024 * 1024
            ),
        )(
            q.reshape(tiles, width), k.reshape(tiles, width), v.reshape(tiles, width),
            tissue, dilation_levels, segment_levels,
        )
        encoded = jnp.dot(out, output_matrix, preferred_element_type=F32).astype(BF16)
        return encoded.reshape(dr, dc, width)

    split = P("row", "col", None)
    return jax.shard_map(
        per_device,
        mesh=mesh,
        in_specs=(split, split, split, P(), P(), P(), P()),
        out_specs=split,
        check_vma=False,
    )
```

```python
import functools
import math

import jax
import jax.numpy as jnp
from jax import lax
from jax.experimental import pallas as pl
from jax.experimental.pallas import tpu as pltpu
from jax.sharding import PartitionSpec as P

HEAD_COUNT = 16
R = 8
DILATION_MIN = 8
NEG_FILL = -1e30
MESH = pl.DeviceIdType.MESH
HEADS_TOGETHER = 4
F32 = jnp.float32
BF16 = jnp.bfloat16


def iota(shape, dim):
    return lax.broadcasted_iota(jnp.int32, shape, dim)


def one_hot(condition):
    return jnp.where(condition, 1.0, 0.0).astype(BF16)


def lane_window(group, head_dimension):
    first = group * HEADS_TOGETHER * head_dimension
    return first // 128 * 128, first % 128


def head_mask(group, head, head_dimension):
    _, offset = lane_window(group, head_dimension)
    lane = iota((1, 256), 1) - offset - head * head_dimension
    return (lane >= 0) & (lane < head_dimension)


def gathered_tissue(tissue, n, key_row, key_col, lanes):
    rows, cols = tissue.shape
    pick = one_hot(iota((n, cols), 1) == key_col(iota((n, cols), 0)))
    by_col = lax.dot_general(
        pick, tissue, (((1,), (1,)), ((), ())), preferred_element_type=F32
    )
    keep = iota((n, rows), 1) == key_row(iota((n, rows), 0))
    kept = jnp.where(keep, by_col, 0.0).astype(BF16)
    return jnp.dot(kept, jnp.ones((rows, lanes), BF16), preferred_element_type=F32)


def window_bias(tissue, n, key_row, key_col, row_offset, column_offset, dr, dc):
    present = gathered_tissue(
        tissue, n, lambda k: key_row(k) + row_offset, lambda k: key_col(k) + column_offset,
        dr * dc,
    )
    k, q = iota((n, dr * dc), 0), iota((n, dr * dc), 1)
    row_gap = jnp.abs(key_row(k) - q // dc)
    col_gap = jnp.abs(key_col(k) - q % dc)
    near = (row_gap <= R) & (col_gap <= R) & (present > 0.5)
    self_key = (row_gap + col_gap) == 0
    return jnp.where(near | self_key, 0.0, NEG_FILL)


def kernel(
    n_row, n_col, dr, dc,
    q_hbm, k_hbm, v_hbm, tissue_ref, dil_ref, seg_ref, out_ref,
    q_ref, query, own_kv, mid_kv, far_kv, halves, chosen, bias_own, bias_mid, bias_far,
    numer, highest, total, local_sem, send_sem, recv_sem, dil_send, dil_recv,
):
    row, col = lax.axis_index("row"), lax.axis_index("col")
    tiles, width = q_ref.shape
    hd = width // HEAD_COUNT
    half = tiles // 2
    corners = 4 * half
    sel = tiles // DILATION_MIN

    loads = [
        pltpu.make_async_copy(k_hbm, own_kv.at[0], local_sem.at[0]),
        pltpu.make_async_copy(v_hbm, own_kv.at[1], local_sem.at[1]),
        pltpu.make_async_copy(q_hbm, q_ref, local_sem.at[2]),
    ]
    for load in loads:
        load.start()

    has_up, has_down = row > 0, row < n_row - 1
    has_left, has_right = col > 0, col < n_col - 1
    up = (lax.rem(row + n_row - 1, n_row), col)
    down = (lax.rem(row + 1, n_row), col)
    left = (row, lax.rem(col + n_col - 1, n_col))
    right = (row, lax.rem(col + 1, n_col))

    barrier = pltpu.get_barrier_semaphore()

    @pl.when(has_up)
    def _():
        pl.semaphore_signal(barrier, inc=1, device_id=up, device_id_type=MESH)

    @pl.when(has_down)
    def _():
        pl.semaphore_signal(barrier, inc=1, device_id=down, device_id_type=MESH)

    @pl.when(has_left)
    def _():
        pl.semaphore_signal(barrier, inc=1, device_id=left, device_id_type=MESH)

    @pl.when(has_right)
    def _():
        pl.semaphore_signal(barrier, inc=1, device_id=right, device_id_type=MESH)

    partner = (row, col + 1 - 2 * (col % 2))
    same_parity = [(row, lax.rem(col + 2 * d, n_col)) for d in range(1, n_col // 2)]
    for peer in same_parity:
        pl.semaphore_signal(barrier, inc=1, device_id=peer, device_id_type=MESH)

    def remote(src, dst, kind, device):
        return pltpu.make_async_remote_copy(
            src_ref=src, dst_ref=dst, send_sem=send_sem.at[kind], recv_sem=recv_sem.at[kind],
            device_id=device, device_id_type=MESH,
        )

    def mid(first, count):
        return mid_kv.at[:, pl.ds(first, count)]

    to_up = remote(own_kv, mid(tiles, tiles), 0, up)
    to_down = remote(own_kv, mid(0, tiles), 1, down)
    to_left, to_right, left_to_up, left_to_down, right_to_up, right_to_down = (
        [], [], [], [], [], []
    )
    for t in range(2):
        left_here = mid_kv.at[t, pl.ds(2 * tiles, half)]
        right_here = mid_kv.at[t, pl.ds(2 * tiles + half, half)]
        corner = [far_kv.at[t, pl.ds(index * half, half)] for index in range(4)]
        sem = 2 + 6 * t
        to_left.append(remote(halves.at[t, pl.ds(0, half)], right_here, sem, left))
        to_right.append(remote(halves.at[t, pl.ds(half, half)], left_here, sem + 1, right))
        left_to_up.append(remote(left_here, corner[2], sem + 2, up))
        left_to_down.append(remote(left_here, corner[0], sem + 3, down))
        right_to_up.append(remote(right_here, corner[3], sem + 4, up))
        right_to_down.append(remote(right_here, corner[1], sem + 5, down))

    i, j = iota((tiles, tiles), 0), iota((tiles, tiles), 1)
    within = i % half
    split_order = one_hot(j == within // R * dc + (i // half) * R + within % R)
    local_sel = dc // DILATION_MIN
    s = i % sel
    phase_order = one_hot(j == s // local_sel * dc + s % local_sel * DILATION_MIN + i // sel)
    lane_phase = iota((1, width), 1) // hd % DILATION_MIN
    pairs = n_col // 2
    own_slot = col % 2 * pairs + col // 2
    slot = pl.ds(pl.multiple_of(corners + own_slot * sel, sel), sel)
    other_slot = (1 - col % 2) * pairs + col // 2
    partner_slot = pl.ds(pl.multiple_of(corners + other_slot * sel, sel), sel)
    parity_slots = pl.ds(pl.multiple_of(corners + col % 2 * pairs * sel, sel), pairs * sel)

    loads[0].wait()
    loads[1].wait()
    for t in range(2):
        halves[t] = jnp.dot(split_order, own_kv[t], preferred_element_type=F32).astype(BF16)
    for t in range(2):
        by_phase = jnp.dot(phase_order, own_kv[t], preferred_element_type=F32)
        picked = jnp.zeros((sel, width), F32)
        for p in range(DILATION_MIN):
            picked += jnp.where(lane_phase == p, by_phase[p * sel:(p + 1) * sel], 0.0)
        picked = picked.astype(BF16)
        chosen[t] = picked
        far_kv[t, slot] = picked
    pl.semaphore_wait(
        barrier,
        len(same_parity)
        + jnp.where(has_up, 1, 0) + jnp.where(has_down, 1, 0)
        + jnp.where(has_left, 1, 0) + jnp.where(has_right, 1, 0),
    )
    def dil_copy(t, src, rows, sem, device):
        return pltpu.make_async_remote_copy(
            src_ref=src, dst_ref=far_kv.at[t, rows],
            send_sem=dil_send.at[sem], recv_sem=dil_recv.at[sem],
            device_id=device, device_id_type=MESH,
        )

    key_spread = [dil_copy(0, chosen.at[0], slot, d, p) for d, p in enumerate(same_parity)]
    value_spread = [
        dil_copy(1, chosen.at[1], slot, pairs + d, p) for d, p in enumerate(same_parity)
    ]
    value_swap = dil_copy(1, chosen.at[1], slot, 2 * pairs, partner)
    value_relay = [
        dil_copy(1, far_kv.at[1, partner_slot], partner_slot, 2 * pairs + 1 + d, p)
        for d, p in enumerate(same_parity)
    ]
    key_swap = dil_copy(0, far_kv.at[0, parity_slots], parity_slots, 3 * pairs + 1, partner)
    value_swap.start()
    for t in range(2):
        pl.when(has_left)(to_left[t].start)
        pl.when(has_right)(to_right[t].start)
    pl.when(has_up)(to_up.start)
    pl.when(has_down)(to_down.start)
    for copy in key_spread + value_spread:
        copy.start()

    def clear(ref, first, count):
        ref[:, pl.ds(first, count)] = jnp.zeros((2, count, width), BF16)

    for ref, first, count, have in (
        (mid_kv, 0, tiles, has_up),
        (mid_kv, tiles, tiles, has_down),
        (mid_kv, 2 * tiles, half, has_left),
        (mid_kv, 2 * tiles + half, half, has_right),
        (far_kv, 0, half, has_up & has_left),
        (far_kv, half, half, has_up & has_right),
        (far_kv, 2 * half, half, has_down & has_left),
        (far_kv, 3 * half, half, has_down & has_right),
    ):
        pl.when(jnp.logical_not(have))(functools.partial(clear, ref, first, count))

    tissue = tissue_ref[...].astype(F32).astype(BF16)
    row_offset, column_offset = row * dr, col * dc

    def bias(n, key_row, key_col):
        return window_bias(tissue, n, key_row, key_col, row_offset, column_offset, dr, dc)

    def half_col(k):
        return jnp.where(k % tiles >= half, dc, -R) + k % R

    bias_own[...] = bias(tiles, lambda k: k // dc, lambda k: k % dc)
    for block, shift in ((0, -dr), (1, dr)):
        bias_mid[pl.ds(block * tiles, tiles)] = bias(
            tiles, lambda k: k // dc + shift, lambda k: k % dc
        )
    bias_mid[pl.ds(2 * tiles, tiles)] = bias(tiles, lambda k: k % half // R, half_col)

    factor = math.log2(math.e) / math.sqrt(hd)
    groups = HEAD_COUNT // HEADS_TOGETHER
    loads[2].wait()
    for g in range(groups):
        base, _ = lane_window(g, hd)
        lanes = q_ref[:, pl.ds(base, 256)]
        for h in range(HEADS_TOGETHER):
            query[g, pl.ds(h * tiles, tiles)] = jnp.where(
                head_mask(g, h, hd), lanes, jnp.zeros_like(lanes)
            )

    def attend(kv, begin, count, extra, first, last):
        values = kv[1, pl.ds(begin, count)].T
        finished = []
        for g in range(groups):
            base, _ = lane_window(g, hd)
            scores = lax.dot_general(
                kv[0, pl.ds(begin, count), pl.ds(base, 256)], query[g], (((1,), (1,)), ((), ())),
                preferred_element_type=F32,
            )
            for h in range(HEADS_TOGETHER):
                head = g * HEADS_TOGETHER + h
                part = scores[:, h * tiles:(h + 1) * tiles] + extra(head)
                top = jnp.max(part, axis=0, keepdims=True)
                if not first:
                    old_top = highest[head]
                    top = jnp.maximum(top, old_top)
                probs = jnp.exp2((part - top) * factor)
                new_total = jnp.sum(probs, axis=0, keepdims=True)
                new_numer = jnp.dot(
                    values[head * hd:(head + 1) * hd], probs.astype(BF16),
                    preferred_element_type=F32,
                )
                if not first:
                    keep = jnp.exp2((old_top - top) * factor)
                    new_total += keep * total[head]
                    new_numer += keep * numer[head]
                if last:
                    finished.append(new_numer * (1.0 / new_total))
                else:
                    highest[head], total[head], numer[head] = top, new_total, new_numer
        return finished

    value_swap.wait_recv()
    for copy in value_relay:
        copy.start()
    attend(own_kv, 0, tiles, lambda head: bias_own[...], True, False)

    for block, shift in ((0, -dr), (1, dr)):
        shared = bias(tiles, lambda k: k % half // R + shift, half_col)
        for h in range(HEAD_COUNT):
            bias_far[h, pl.ds(block * tiles, tiles)] = shared
    n_dil = sel * n_col

    def dil_row(k):
        return k % sel // local_sel

    def dil_col(k):
        place = k // sel
        device = place % pairs * 2 + place // pairs
        return device * dc + k % local_sel * DILATION_MIN

    k, q = iota((n_dil, tiles), 0), iota((n_dil, tiles), 1)
    same_row = dil_row(k) == q // dc
    for p in range(DILATION_MIN):
        present = gathered_tissue(
            tissue, n_dil, lambda k: dil_row(k) + row_offset, lambda k: dil_col(k) + p, tiles
        )
        allowed = same_row & (present > 0.5)
        key_col = dil_col(k) + p
        apart = key_col ^ (column_offset + q % dc)
        for head in range(p, HEAD_COUNT, DILATION_MIN):
            stride = jnp.left_shift(jnp.int32(DILATION_MIN), dil_ref[head])
            segment = jnp.right_shift(jnp.int32(dc * n_col), seg_ref[head])
            phase_ok = ((key_col ^ head) & (stride - 1)) == 0
            ok = allowed & phase_ok & (apart < segment)
            bias_far[head, pl.ds(corners, n_dil)] = jnp.where(ok, 0.0, NEG_FILL)

    pl.when(has_down)(to_up.wait_recv)
    pl.when(has_up)(to_down.wait_recv)
    attend(mid_kv, 0, 2 * tiles, lambda head: bias_mid[pl.ds(0, 2 * tiles)], False, False)

    for t in range(2):

        @pl.when(has_left)
        def _(t=t):
            to_right[t].wait_recv()
            pl.when(has_up)(left_to_up[t].start)
            pl.when(has_down)(left_to_down[t].start)

        @pl.when(has_right)
        def _(t=t):
            to_left[t].wait_recv()
            pl.when(has_up)(right_to_up[t].start)
            pl.when(has_down)(right_to_down[t].start)

    for copy in key_spread:
        copy.wait_recv()
    key_swap.start()

    attend(
        mid_kv, 2 * tiles, tiles, lambda head: bias_mid[pl.ds(2 * tiles, tiles)], False, False
    )
    for copy in [key_swap] + value_spread + value_relay:
        copy.wait_recv()
    for t in range(2):
        pl.when(has_left & has_up)(left_to_down[t].wait_recv)
        pl.when(has_left & has_down)(left_to_up[t].wait_recv)
        pl.when(has_right & has_up)(right_to_down[t].wait_recv)
        pl.when(has_right & has_down)(right_to_up[t].wait_recv)

    finished = attend(
        far_kv, 0, corners + n_dil, lambda head: bias_far[head], False, True
    )
    out_ref[...] = jnp.concatenate(finished, axis=0).T.astype(BF16)

    pl.when(has_up)(to_up.wait_send)
    pl.when(has_down)(to_down.wait_send)
    for t in range(2):
        pl.when(has_left)(to_left[t].wait_send)
        pl.when(has_right)(to_right[t].wait_send)
        pl.when(has_left & has_up)(left_to_up[t].wait_send)
        pl.when(has_left & has_down)(left_to_down[t].wait_send)
        pl.when(has_right & has_up)(right_to_up[t].wait_send)
        pl.when(has_right & has_down)(right_to_down[t].wait_send)
    for copy in key_spread + value_spread + value_relay + [value_swap, key_swap]:
        copy.wait_send()


def solution(mesh):
    n_row, n_col = mesh.shape["row"], mesh.shape["col"]

    def per_device(q, k, v, tissue, dilation_levels, segment_levels, output_matrix):
        dr, dc, width = q.shape
        tiles = dr * dc
        sel = tiles // DILATION_MIN
        groups = HEAD_COUNT // HEADS_TOGETHER
        hbm = pl.BlockSpec(memory_space=pltpu.HBM)
        vmem = pl.BlockSpec(memory_space=pltpu.VMEM)
        smem = pl.BlockSpec(memory_space=pltpu.SMEM)
        out = pl.pallas_call(
            functools.partial(kernel, n_row, n_col, dr, dc),
            out_shape=jax.ShapeDtypeStruct((tiles, width), BF16),
            in_specs=[hbm, hbm, hbm, vmem, smem, smem],
            out_specs=vmem,
            scratch_shapes=[
                pltpu.VMEM((tiles, width), BF16),
                pltpu.VMEM((groups, HEADS_TOGETHER * tiles, 256), BF16),
                pltpu.VMEM((2, tiles, width), BF16),
                pltpu.VMEM((2, 3 * tiles, width), BF16),
                pltpu.VMEM((2, 2 * tiles + sel * n_col, width), BF16),
                pltpu.VMEM((2, tiles, width), BF16),
                pltpu.VMEM((2, sel, width), BF16),
                pltpu.VMEM((tiles, tiles), F32),
                pltpu.VMEM((3 * tiles, tiles), F32),
                pltpu.VMEM((HEAD_COUNT, 2 * tiles + sel * n_col, tiles), F32),
                pltpu.VMEM((HEAD_COUNT, width // HEAD_COUNT, tiles), F32),
                pltpu.VMEM((HEAD_COUNT, 1, tiles), F32),
                pltpu.VMEM((HEAD_COUNT, 1, tiles), F32),
                pltpu.SemaphoreType.DMA((3,)),
                pltpu.SemaphoreType.DMA((14,)),
                pltpu.SemaphoreType.DMA((14,)),
                pltpu.SemaphoreType.DMA((2 * n_col,)),
                pltpu.SemaphoreType.DMA((2 * n_col,)),
            ],
            compiler_params=pltpu.CompilerParams(
                collective_id=0, has_side_effects=True, vmem_limit_bytes=56 * 1024 * 1024
            ),
        )(
            q.reshape(tiles, width), k.reshape(tiles, width), v.reshape(tiles, width),
            tissue, dilation_levels, segment_levels,
        )
        encoded = jnp.dot(out, output_matrix, preferred_element_type=F32).astype(BF16)
        return encoded.reshape(dr, dc, width)

    split = P("row", "col", None)
    return jax.shard_map(
        per_device,
        mesh=mesh,
        in_specs=(split, split, split, P(), P(), P(), P()),
        out_specs=split,
        check_vma=False,
    )
```

```python
import functools
import math

import jax
import jax.numpy as jnp
from jax import lax
from jax.experimental import pallas as pl
from jax.experimental.pallas import tpu as pltpu
from jax.sharding import PartitionSpec as P

HEAD_COUNT = 16
R = 8
DILATION_MIN = 8
NEG_FILL = -1e30
MESH = pl.DeviceIdType.MESH
HEADS_TOGETHER = 4
F32 = jnp.float32
BF16 = jnp.bfloat16


def iota(shape, dim):
    return lax.broadcasted_iota(jnp.int32, shape, dim)


def one_hot(condition):
    return jnp.where(condition, 1.0, 0.0).astype(BF16)


def lane_window(group, head_dimension):
    first = group * HEADS_TOGETHER * head_dimension
    return first // 128 * 128, first % 128


def head_mask(group, head, head_dimension):
    _, offset = lane_window(group, head_dimension)
    lane = iota((1, 256), 1) - offset - head * head_dimension
    return (lane >= 0) & (lane < head_dimension)


def gathered_tissue(tissue, n, key_row, key_col, lanes):
    rows, cols = tissue.shape
    pick = one_hot(iota((n, cols), 1) == key_col(iota((n, cols), 0)))
    by_col = lax.dot_general(
        pick, tissue, (((1,), (1,)), ((), ())), preferred_element_type=F32
    )
    keep = iota((n, rows), 1) == key_row(iota((n, rows), 0))
    kept = jnp.where(keep, by_col, 0.0).astype(BF16)
    return jnp.dot(kept, jnp.ones((rows, lanes), BF16), preferred_element_type=F32)


def window_bias(tissue, n, key_row, key_col, row_offset, column_offset, dr, dc):
    present = gathered_tissue(
        tissue, n, lambda k: key_row(k) + row_offset, lambda k: key_col(k) + column_offset,
        dr * dc,
    )
    k, q = iota((n, dr * dc), 0), iota((n, dr * dc), 1)
    row_gap = jnp.abs(key_row(k) - q // dc)
    col_gap = jnp.abs(key_col(k) - q % dc)
    near = (row_gap <= R) & (col_gap <= R) & (present > 0.5)
    self_key = (row_gap + col_gap) == 0
    return jnp.where(near | self_key, 0.0, NEG_FILL)


def kernel(
    n_row, n_col, dr, dc,
    q_hbm, k_hbm, v_hbm, tissue_ref, dil_ref, seg_ref, out_ref,
    q_ref, query, own_kv, mid_kv, far_kv, halves, chosen, bias_own, bias_mid, bias_far,
    numer, highest, total, local_sem, send_sem, recv_sem, dil_send, dil_recv,
):
    row, col = lax.axis_index("row"), lax.axis_index("col")
    tiles, width = q_ref.shape
    hd = width // HEAD_COUNT
    half = tiles // 2
    corners = 4 * half
    sel = tiles // DILATION_MIN

    loads = [
        pltpu.make_async_copy(k_hbm, own_kv.at[0], local_sem.at[0]),
        pltpu.make_async_copy(v_hbm, own_kv.at[1], local_sem.at[1]),
        pltpu.make_async_copy(q_hbm, q_ref, local_sem.at[2]),
    ]
    for load in loads:
        load.start()

    has_up, has_down = row > 0, row < n_row - 1
    has_left, has_right = col > 0, col < n_col - 1
    even, odd = row % 2 == 0, row % 2 == 1
    up = (lax.rem(row + n_row - 1, n_row), col)
    down = (lax.rem(row + 1, n_row), col)
    left = (row, lax.rem(col + n_col - 1, n_col))
    right = (row, lax.rem(col + 1, n_col))

    barrier = pltpu.get_barrier_semaphore()

    @pl.when(has_up)
    def _():
        pl.semaphore_signal(barrier, inc=1, device_id=up, device_id_type=MESH)

    @pl.when(has_down)
    def _():
        pl.semaphore_signal(barrier, inc=1, device_id=down, device_id_type=MESH)

    @pl.when(has_left)
    def _():
        pl.semaphore_signal(barrier, inc=1, device_id=left, device_id_type=MESH)

    @pl.when(has_right)
    def _():
        pl.semaphore_signal(barrier, inc=1, device_id=right, device_id_type=MESH)

    partner = (row, col + 1 - 2 * (col % 2))
    same_parity = [(row, lax.rem(col + 2 * d, n_col)) for d in range(1, n_col // 2)]
    for peer in same_parity:
        pl.semaphore_signal(barrier, inc=1, device_id=peer, device_id_type=MESH)

    def remote(src, dst, kind, device):
        return pltpu.make_async_remote_copy(
            src_ref=src, dst_ref=dst, send_sem=send_sem.at[kind], recv_sem=recv_sem.at[kind],
            device_id=device, device_id_type=MESH,
        )

    def mid(first, count):
        return mid_kv.at[:, pl.ds(first, count)]

    to_up = remote(own_kv, mid(tiles, tiles), 0, up)
    to_down = remote(own_kv, mid(0, tiles), 1, down)
    to_left, to_right, left_to_up, left_to_down, right_to_up, right_to_down = (
        [], [], [], [], [], []
    )
    for t in range(2):
        left_here = mid_kv.at[t, pl.ds(2 * tiles, half)]
        right_here = mid_kv.at[t, pl.ds(2 * tiles + half, half)]
        corner = [far_kv.at[t, pl.ds(index * half, half)] for index in range(4)]
        sem = 2 + 6 * t
        to_left.append(remote(halves.at[t, pl.ds(0, half)], right_here, sem, left))
        to_right.append(remote(halves.at[t, pl.ds(half, half)], left_here, sem + 1, right))
        left_to_up.append(remote(left_here, corner[2], sem + 2, up))
        left_to_down.append(remote(left_here, corner[0], sem + 3, down))
        right_to_up.append(remote(right_here, corner[3], sem + 4, up))
        right_to_down.append(remote(right_here, corner[1], sem + 5, down))

    i, j = iota((tiles, tiles), 0), iota((tiles, tiles), 1)
    within = i % half
    split_order = one_hot(j == within // R * dc + (i // half) * R + within % R)
    local_sel = dc // DILATION_MIN
    s = i % sel
    phase_order = one_hot(j == s // local_sel * dc + s % local_sel * DILATION_MIN + i // sel)
    lane_phase = iota((1, width), 1) // hd % DILATION_MIN
    pairs = n_col // 2
    own_slot = col % 2 * pairs + col // 2
    slot = pl.ds(pl.multiple_of(corners + own_slot * sel, sel), sel)
    other_slot = (1 - col % 2) * pairs + col // 2
    partner_slot = pl.ds(pl.multiple_of(corners + other_slot * sel, sel), sel)
    parity_slots = pl.ds(pl.multiple_of(corners + col % 2 * pairs * sel, sel), pairs * sel)

    loads[0].wait()
    loads[1].wait()
    for t in range(2):
        halves[t] = jnp.dot(split_order, own_kv[t], preferred_element_type=F32).astype(BF16)
    for t in range(2):
        by_phase = jnp.dot(phase_order, own_kv[t], preferred_element_type=F32)
        picked = jnp.zeros((sel, width), F32)
        for p in range(DILATION_MIN):
            picked += jnp.where(lane_phase == p, by_phase[p * sel:(p + 1) * sel], 0.0)
        picked = picked.astype(BF16)
        chosen[t] = picked
        far_kv[t, slot] = picked
    pl.semaphore_wait(
        barrier,
        len(same_parity)
        + jnp.where(has_up, 1, 0) + jnp.where(has_down, 1, 0)
        + jnp.where(has_left, 1, 0) + jnp.where(has_right, 1, 0),
    )
    def dil_copy(t, src, rows, sem, device):
        return pltpu.make_async_remote_copy(
            src_ref=src, dst_ref=far_kv.at[t, rows],
            send_sem=dil_send.at[sem], recv_sem=dil_recv.at[sem],
            device_id=device, device_id_type=MESH,
        )

    key_spread = [dil_copy(0, chosen.at[0], slot, d, p) for d, p in enumerate(same_parity)]
    value_spread = [
        dil_copy(1, chosen.at[1], slot, pairs + d, p) for d, p in enumerate(same_parity)
    ]
    value_swap = dil_copy(1, chosen.at[1], slot, 2 * pairs, partner)
    value_relay = [
        dil_copy(1, far_kv.at[1, partner_slot], partner_slot, 2 * pairs + 1 + d, p)
        for d, p in enumerate(same_parity)
    ]
    key_swap = dil_copy(0, far_kv.at[0, parity_slots], parity_slots, 3 * pairs + 1, partner)
    value_swap.start()
    for t in range(2):
        pl.when(has_left)(to_left[t].start)
        pl.when(has_right)(to_right[t].start)
        if t == 0:
            pl.when(has_up & even)(to_up.start)
            pl.when(has_down & odd)(to_down.start)
    pl.when(has_up & odd)(to_up.start)
    pl.when(has_down & even)(to_down.start)
    for copy in key_spread + value_spread:
        copy.start()

    def clear(ref, first, count):
        ref[:, pl.ds(first, count)] = jnp.zeros((2, count, width), BF16)

    for ref, first, count, have in (
        (mid_kv, 0, tiles, has_up),
        (mid_kv, tiles, tiles, has_down),
        (mid_kv, 2 * tiles, half, has_left),
        (mid_kv, 2 * tiles + half, half, has_right),
        (far_kv, 0, half, has_up & has_left),
        (far_kv, half, half, has_up & has_right),
        (far_kv, 2 * half, half, has_down & has_left),
        (far_kv, 3 * half, half, has_down & has_right),
    ):
        pl.when(jnp.logical_not(have))(functools.partial(clear, ref, first, count))

    tissue = tissue_ref[...].astype(F32).astype(BF16)
    row_offset, column_offset = row * dr, col * dc

    def bias(n, key_row, key_col):
        return window_bias(tissue, n, key_row, key_col, row_offset, column_offset, dr, dc)

    def half_col(k):
        return jnp.where(k % tiles >= half, dc, -R) + k % R

    bias_own[...] = bias(tiles, lambda k: k // dc, lambda k: k % dc)
    for block, shift in ((0, -dr), (1, dr)):
        bias_mid[pl.ds(block * tiles, tiles)] = bias(
            tiles, lambda k: k // dc + shift, lambda k: k % dc
        )
    bias_mid[pl.ds(2 * tiles, tiles)] = bias(tiles, lambda k: k % half // R, half_col)

    factor = math.log2(math.e) / math.sqrt(hd)
    groups = HEAD_COUNT // HEADS_TOGETHER
    loads[2].wait()
    for g in range(groups):
        base, _ = lane_window(g, hd)
        lanes = q_ref[:, pl.ds(base, 256)]
        for h in range(HEADS_TOGETHER):
            query[g, pl.ds(h * tiles, tiles)] = jnp.where(
                head_mask(g, h, hd), lanes, jnp.zeros_like(lanes)
            )

    def attend(kv, begin, count, extra, first, last):
        values = kv[1, pl.ds(begin, count)].T
        finished = []
        for g in range(groups):
            base, _ = lane_window(g, hd)
            scores = lax.dot_general(
                kv[0, pl.ds(begin, count), pl.ds(base, 256)], query[g], (((1,), (1,)), ((), ())),
                preferred_element_type=F32,
            )
            for h in range(HEADS_TOGETHER):
                head = g * HEADS_TOGETHER + h
                part = scores[:, h * tiles:(h + 1) * tiles] + extra(head)
                top = jnp.max(part, axis=0, keepdims=True)
                if not first:
                    old_top = highest[head]
                    top = jnp.maximum(top, old_top)
                probs = jnp.exp2((part - top) * factor)
                new_total = jnp.sum(probs, axis=0, keepdims=True)
                new_numer = jnp.dot(
                    values[head * hd:(head + 1) * hd], probs.astype(BF16),
                    preferred_element_type=F32,
                )
                if not first:
                    keep = jnp.exp2((old_top - top) * factor)
                    new_total += keep * total[head]
                    new_numer += keep * numer[head]
                if last:
                    finished.append(new_numer * (1.0 / new_total))
                else:
                    highest[head], total[head], numer[head] = top, new_total, new_numer
        return finished

    value_swap.wait_recv()
    for copy in value_relay:
        copy.start()
    attend(own_kv, 0, tiles, lambda head: bias_own[...], True, False)

    for block, shift in ((0, -dr), (1, dr)):
        shared = bias(tiles, lambda k: k % half // R + shift, half_col)
        for h in range(HEAD_COUNT):
            bias_far[h, pl.ds(block * tiles, tiles)] = shared
    n_dil = sel * n_col

    def dil_row(k):
        return k % sel // local_sel

    def dil_col(k):
        place = k // sel
        device = place % pairs * 2 + place // pairs
        return device * dc + k % local_sel * DILATION_MIN

    k, q = iota((n_dil, tiles), 0), iota((n_dil, tiles), 1)
    same_row = dil_row(k) == q // dc
    for p in range(DILATION_MIN):
        present = gathered_tissue(
            tissue, n_dil, lambda k: dil_row(k) + row_offset, lambda k: dil_col(k) + p, tiles
        )
        allowed = same_row & (present > 0.5)
        key_col = dil_col(k) + p
        apart = key_col ^ (column_offset + q % dc)
        for head in range(p, HEAD_COUNT, DILATION_MIN):
            stride = jnp.left_shift(jnp.int32(DILATION_MIN), dil_ref[head])
            segment = jnp.right_shift(jnp.int32(dc * n_col), seg_ref[head])
            phase_ok = ((key_col ^ head) & (stride - 1)) == 0
            ok = allowed & phase_ok & (apart < segment)
            bias_far[head, pl.ds(corners, n_dil)] = jnp.where(ok, 0.0, NEG_FILL)

    pl.when(has_down)(to_up.wait_recv)
    pl.when(has_up)(to_down.wait_recv)
    attend(mid_kv, 0, 2 * tiles, lambda head: bias_mid[pl.ds(0, 2 * tiles)], False, False)

    for t in range(2):
        for have, arrived, upward, downward in (
            (has_left, to_right[t], left_to_up[t], left_to_down[t]),
            (has_right, to_left[t], right_to_up[t], right_to_down[t]),
        ):
            pl.when(have)(arrived.wait_recv)
            pl.when(have & has_up & even)(upward.start)
            pl.when(have & has_down)(downward.start)
            pl.when(have & has_up & odd)(upward.start)

    for copy in key_spread:
        copy.wait_recv()
    key_swap.start()

    attend(
        mid_kv, 2 * tiles, tiles, lambda head: bias_mid[pl.ds(2 * tiles, tiles)], False, False
    )
    def corners_arrived(from_up, from_down):
        for t in range(2):
            pl.when(has_left & has_up & from_up)(left_to_down[t].wait_recv)
            pl.when(has_right & has_up & from_up)(right_to_down[t].wait_recv)
            pl.when(has_left & has_down & from_down)(left_to_up[t].wait_recv)
            pl.when(has_right & has_down & from_down)(right_to_up[t].wait_recv)

    def far_stage(begin, count, last):
        return attend(
            far_kv, begin, count, lambda head: bias_far[head, pl.ds(begin, count)], False, last
        )

    corners_arrived(odd, even)
    far_stage(pl.multiple_of((1 - row % 2) * tiles, tiles), tiles, False)
    for copy in [key_swap] + value_spread + value_relay:
        copy.wait_recv()
    far_stage(corners, n_dil, False)
    corners_arrived(even, odd)
    finished = far_stage(pl.multiple_of(row % 2 * tiles, tiles), tiles, True)
    out_ref[...] = jnp.concatenate(finished, axis=0).T.astype(BF16)

    pl.when(has_up)(to_up.wait_send)
    pl.when(has_down)(to_down.wait_send)
    for t in range(2):
        pl.when(has_left)(to_left[t].wait_send)
        pl.when(has_right)(to_right[t].wait_send)
        pl.when(has_left & has_up)(left_to_up[t].wait_send)
        pl.when(has_left & has_down)(left_to_down[t].wait_send)
        pl.when(has_right & has_up)(right_to_up[t].wait_send)
        pl.when(has_right & has_down)(right_to_down[t].wait_send)
    for copy in key_spread + value_spread + value_relay + [value_swap, key_swap]:
        copy.wait_send()


def solution(mesh):
    n_row, n_col = mesh.shape["row"], mesh.shape["col"]

    def per_device(q, k, v, tissue, dilation_levels, segment_levels, output_matrix):
        dr, dc, width = q.shape
        tiles = dr * dc
        sel = tiles // DILATION_MIN
        groups = HEAD_COUNT // HEADS_TOGETHER
        hbm = pl.BlockSpec(memory_space=pltpu.HBM)
        vmem = pl.BlockSpec(memory_space=pltpu.VMEM)
        smem = pl.BlockSpec(memory_space=pltpu.SMEM)
        out = pl.pallas_call(
            functools.partial(kernel, n_row, n_col, dr, dc),
            out_shape=jax.ShapeDtypeStruct((tiles, width), BF16),
            in_specs=[hbm, hbm, hbm, vmem, smem, smem],
            out_specs=vmem,
            scratch_shapes=[
                pltpu.VMEM((tiles, width), BF16),
                pltpu.VMEM((groups, HEADS_TOGETHER * tiles, 256), BF16),
                pltpu.VMEM((2, tiles, width), BF16),
                pltpu.VMEM((2, 3 * tiles, width), BF16),
                pltpu.VMEM((2, 2 * tiles + sel * n_col, width), BF16),
                pltpu.VMEM((2, tiles, width), BF16),
                pltpu.VMEM((2, sel, width), BF16),
                pltpu.VMEM((tiles, tiles), F32),
                pltpu.VMEM((3 * tiles, tiles), F32),
                pltpu.VMEM((HEAD_COUNT, 2 * tiles + sel * n_col, tiles), F32),
                pltpu.VMEM((HEAD_COUNT, width // HEAD_COUNT, tiles), F32),
                pltpu.VMEM((HEAD_COUNT, 1, tiles), F32),
                pltpu.VMEM((HEAD_COUNT, 1, tiles), F32),
                pltpu.SemaphoreType.DMA((3,)),
                pltpu.SemaphoreType.DMA((14,)),
                pltpu.SemaphoreType.DMA((14,)),
                pltpu.SemaphoreType.DMA((2 * n_col,)),
                pltpu.SemaphoreType.DMA((2 * n_col,)),
            ],
            compiler_params=pltpu.CompilerParams(
                collective_id=0, has_side_effects=True, vmem_limit_bytes=56 * 1024 * 1024
            ),
        )(
            q.reshape(tiles, width), k.reshape(tiles, width), v.reshape(tiles, width),
            tissue, dilation_levels, segment_levels,
        )
        encoded = jnp.dot(out, output_matrix, preferred_element_type=F32).astype(BF16)
        return encoded.reshape(dr, dc, width)

    split = P("row", "col", None)
    return jax.shard_map(
        per_device,
        mesh=mesh,
        in_specs=(split, split, split, P(), P(), P(), P()),
        out_specs=split,
        check_vma=False,
    )
```

```python
import functools
import math

import jax
import jax.numpy as jnp
from jax import lax
from jax.experimental import pallas as pl
from jax.experimental.pallas import tpu as pltpu
from jax.sharding import PartitionSpec as P

HEAD_COUNT = 16
R = 8
DILATION_MIN = 8
NEG_FILL = -1e30
MESH = pl.DeviceIdType.MESH
HEADS_TOGETHER = 4
F32 = jnp.float32
BF16 = jnp.bfloat16


def iota(shape, dim):
    return lax.broadcasted_iota(jnp.int32, shape, dim)


def one_hot(condition):
    return jnp.where(condition, 1.0, 0.0).astype(BF16)


def lane_window(group, head_dimension):
    first = group * HEADS_TOGETHER * head_dimension
    return first // 128 * 128, first % 128


def head_mask(group, head, head_dimension):
    _, offset = lane_window(group, head_dimension)
    lane = iota((1, 256), 1) - offset - head * head_dimension
    return (lane >= 0) & (lane < head_dimension)


def gathered_tissue(tissue, n, key_row, key_col, lanes):
    rows, cols = tissue.shape
    pick = one_hot(iota((n, cols), 1) == key_col(iota((n, cols), 0)))
    by_col = lax.dot_general(
        pick, tissue, (((1,), (1,)), ((), ())), preferred_element_type=F32
    )
    keep = iota((n, rows), 1) == key_row(iota((n, rows), 0))
    kept = jnp.where(keep, by_col, 0.0).astype(BF16)
    return jnp.dot(kept, jnp.ones((rows, lanes), BF16), preferred_element_type=F32)


def window_bias(tissue, n, key_row, key_col, row_offset, column_offset, dr, dc):
    present = gathered_tissue(
        tissue, n, lambda k: key_row(k) + row_offset, lambda k: key_col(k) + column_offset,
        dr * dc,
    )
    k, q = iota((n, dr * dc), 0), iota((n, dr * dc), 1)
    row_gap = jnp.abs(key_row(k) - q // dc)
    col_gap = jnp.abs(key_col(k) - q % dc)
    near = (row_gap <= R) & (col_gap <= R) & (present > 0.5)
    self_key = (row_gap + col_gap) == 0
    return jnp.where(near | self_key, 0.0, NEG_FILL)


def kernel(
    n_row, n_col, dr, dc,
    q_hbm, k_hbm, v_hbm, tissue_ref, dil_ref, seg_ref, out_ref,
    q_ref, query, own_kv, mid_kv, far_kv, halves, chosen, bias_own, bias_mid, bias_far,
    numer, highest, total, local_sem, send_sem, recv_sem, dil_send, dil_recv,
):
    row, col = lax.axis_index("row"), lax.axis_index("col")
    tiles, width = q_ref.shape
    hd = width // HEAD_COUNT
    half = tiles // 2
    corners = 4 * half
    sel = tiles // DILATION_MIN

    loads = [
        pltpu.make_async_copy(k_hbm, own_kv.at[0], local_sem.at[0]),
        pltpu.make_async_copy(v_hbm, own_kv.at[1], local_sem.at[1]),
        pltpu.make_async_copy(q_hbm, q_ref, local_sem.at[2]),
    ]
    for load in loads:
        load.start()

    has_up, has_down = row > 0, row < n_row - 1
    has_left, has_right = col > 0, col < n_col - 1
    even, odd = row % 2 == 0, row % 2 == 1
    up = (lax.rem(row + n_row - 1, n_row), col)
    down = (lax.rem(row + 1, n_row), col)
    left = (row, lax.rem(col + n_col - 1, n_col))
    right = (row, lax.rem(col + 1, n_col))

    barrier = pltpu.get_barrier_semaphore()

    @pl.when(has_up)
    def _():
        pl.semaphore_signal(barrier, inc=1, device_id=up, device_id_type=MESH)

    @pl.when(has_down)
    def _():
        pl.semaphore_signal(barrier, inc=1, device_id=down, device_id_type=MESH)

    @pl.when(has_left)
    def _():
        pl.semaphore_signal(barrier, inc=1, device_id=left, device_id_type=MESH)

    @pl.when(has_right)
    def _():
        pl.semaphore_signal(barrier, inc=1, device_id=right, device_id_type=MESH)

    partner = (row, col + 1 - 2 * (col % 2))
    same_parity = [(row, lax.rem(col + 2 * d, n_col)) for d in range(1, n_col // 2)]
    for peer in same_parity:
        pl.semaphore_signal(barrier, inc=1, device_id=peer, device_id_type=MESH)

    def remote(src, dst, kind, device):
        return pltpu.make_async_remote_copy(
            src_ref=src, dst_ref=dst, send_sem=send_sem.at[kind], recv_sem=recv_sem.at[kind],
            device_id=device, device_id_type=MESH,
        )

    def mid(first, count):
        return mid_kv.at[:, pl.ds(first, count)]

    to_up = remote(own_kv, mid(tiles, tiles), 0, up)
    to_down = remote(own_kv, mid(0, tiles), 1, down)
    to_left, to_right, left_to_up, left_to_down, right_to_up, right_to_down = (
        [], [], [], [], [], []
    )
    piece = half // 2
    pieces = range(4)
    for n in pieces:
        t, skip = n // 2, n % 2 * piece
        left_here = mid_kv.at[t, pl.ds(2 * tiles + skip, piece)]
        right_here = mid_kv.at[t, pl.ds(2 * tiles + half + skip, piece)]
        corner = [far_kv.at[t, pl.ds(index * half + skip, piece)] for index in range(4)]
        sem = 2 + 6 * n
        to_left.append(remote(halves.at[t, pl.ds(skip, piece)], right_here, sem, left))
        to_right.append(remote(halves.at[t, pl.ds(half + skip, piece)], left_here, sem + 1, right))
        left_to_up.append(remote(left_here, corner[2], sem + 2, up))
        left_to_down.append(remote(left_here, corner[0], sem + 3, down))
        right_to_up.append(remote(right_here, corner[3], sem + 4, up))
        right_to_down.append(remote(right_here, corner[1], sem + 5, down))

    i, j = iota((tiles, tiles), 0), iota((tiles, tiles), 1)
    within = i % half
    split_order = one_hot(j == within // R * dc + (i // half) * R + within % R)
    local_sel = dc // DILATION_MIN
    s = i % sel
    phase_order = one_hot(j == s // local_sel * dc + s % local_sel * DILATION_MIN + i // sel)
    lane_phase = iota((1, width), 1) // hd % DILATION_MIN
    pairs = n_col // 2
    own_slot = col % 2 * pairs + col // 2
    slot = pl.ds(pl.multiple_of(corners + own_slot * sel, sel), sel)
    other_slot = (1 - col % 2) * pairs + col // 2
    partner_slot = pl.ds(pl.multiple_of(corners + other_slot * sel, sel), sel)
    parity_slots = pl.ds(pl.multiple_of(corners + col % 2 * pairs * sel, sel), pairs * sel)

    loads[0].wait()
    loads[1].wait()
    for t in range(2):
        halves[t] = jnp.dot(split_order, own_kv[t], preferred_element_type=F32).astype(BF16)
    for t in range(2):
        by_phase = jnp.dot(phase_order, own_kv[t], preferred_element_type=F32)
        picked = jnp.zeros((sel, width), F32)
        for p in range(DILATION_MIN):
            picked += jnp.where(lane_phase == p, by_phase[p * sel:(p + 1) * sel], 0.0)
        picked = picked.astype(BF16)
        chosen[t] = picked
        far_kv[t, slot] = picked
    pl.semaphore_wait(
        barrier,
        len(same_parity)
        + jnp.where(has_up, 1, 0) + jnp.where(has_down, 1, 0)
        + jnp.where(has_left, 1, 0) + jnp.where(has_right, 1, 0),
    )
    def dil_copy(t, src, rows, sem, device):
        return pltpu.make_async_remote_copy(
            src_ref=src, dst_ref=far_kv.at[t, rows],
            send_sem=dil_send.at[sem], recv_sem=dil_recv.at[sem],
            device_id=device, device_id_type=MESH,
        )

    key_spread = [dil_copy(0, chosen.at[0], slot, d, p) for d, p in enumerate(same_parity)]
    value_spread = [
        dil_copy(1, chosen.at[1], slot, pairs + d, p) for d, p in enumerate(same_parity)
    ]
    value_swap = dil_copy(1, chosen.at[1], slot, 2 * pairs, partner)
    value_relay = [
        dil_copy(1, far_kv.at[1, partner_slot], partner_slot, 2 * pairs + 1 + d, p)
        for d, p in enumerate(same_parity)
    ]
    key_swap = dil_copy(0, far_kv.at[0, parity_slots], parity_slots, 3 * pairs + 1, partner)
    value_swap.start()
    for t in pieces:
        pl.when(has_left)(to_left[t].start)
        pl.when(has_right)(to_right[t].start)
        if t == 1:
            pl.when(has_up & even)(to_up.start)
            pl.when(has_down & odd)(to_down.start)
    pl.when(has_up & odd)(to_up.start)
    pl.when(has_down & even)(to_down.start)
    for copy in key_spread + value_spread:
        copy.start()

    def clear(ref, first, count):
        ref[:, pl.ds(first, count)] = jnp.zeros((2, count, width), BF16)

    for ref, first, count, have in (
        (mid_kv, 0, tiles, has_up),
        (mid_kv, tiles, tiles, has_down),
        (mid_kv, 2 * tiles, half, has_left),
        (mid_kv, 2 * tiles + half, half, has_right),
        (far_kv, 0, half, has_up & has_left),
        (far_kv, half, half, has_up & has_right),
        (far_kv, 2 * half, half, has_down & has_left),
        (far_kv, 3 * half, half, has_down & has_right),
    ):
        pl.when(jnp.logical_not(have))(functools.partial(clear, ref, first, count))

    tissue = tissue_ref[...].astype(F32).astype(BF16)
    row_offset, column_offset = row * dr, col * dc

    def bias(n, key_row, key_col):
        return window_bias(tissue, n, key_row, key_col, row_offset, column_offset, dr, dc)

    def half_col(k):
        return jnp.where(k % tiles >= half, dc, -R) + k % R

    bias_own[...] = bias(tiles, lambda k: k // dc, lambda k: k % dc)
    for block, shift in ((0, -dr), (1, dr)):
        bias_mid[pl.ds(block * tiles, tiles)] = bias(
            tiles, lambda k: k // dc + shift, lambda k: k % dc
        )
    bias_mid[pl.ds(2 * tiles, tiles)] = bias(tiles, lambda k: k % half // R, half_col)

    factor = math.log2(math.e) / math.sqrt(hd)
    groups = HEAD_COUNT // HEADS_TOGETHER
    loads[2].wait()
    for g in range(groups):
        base, _ = lane_window(g, hd)
        lanes = q_ref[:, pl.ds(base, 256)]
        for h in range(HEADS_TOGETHER):
            query[g, pl.ds(h * tiles, tiles)] = jnp.where(
                head_mask(g, h, hd), lanes, jnp.zeros_like(lanes)
            )

    def attend(kv, begin, count, extra, first):
        values = kv[1, pl.ds(begin, count)].T
        for g in range(groups):
            base, _ = lane_window(g, hd)
            scores = lax.dot_general(
                kv[0, pl.ds(begin, count), pl.ds(base, 256)], query[g], (((1,), (1,)), ((), ())),
                preferred_element_type=F32,
            )
            for h in range(HEADS_TOGETHER):
                head = g * HEADS_TOGETHER + h
                part = scores[:, h * tiles:(h + 1) * tiles] + extra(head)
                top = jnp.max(part, axis=0, keepdims=True)
                if not first:
                    old_top = highest[head]
                    top = jnp.maximum(top, old_top)
                probs = jnp.exp2((part - top) * factor)
                new_total = jnp.sum(probs, axis=0, keepdims=True)
                new_numer = jnp.dot(
                    values[head * hd:(head + 1) * hd], probs.astype(BF16),
                    preferred_element_type=F32,
                )
                if not first:
                    keep = jnp.exp2((old_top - top) * factor)
                    new_total += keep * total[head]
                    new_numer += keep * numer[head]
                highest[head], total[head], numer[head] = top, new_total, new_numer

    value_swap.wait_recv()
    for copy in value_relay:
        copy.start()
    attend(own_kv, 0, tiles, lambda head: bias_own[...], True)

    for block, shift in ((0, -dr), (1, dr)):
        shared = bias(tiles, lambda k: k % half // R + shift, half_col)
        for h in range(HEAD_COUNT):
            bias_far[h, pl.ds(block * tiles, tiles)] = shared
    n_dil = sel * n_col

    def dil_row(k):
        return k % sel // local_sel

    def dil_col(k):
        place = k // sel
        device = place % pairs * 2 + place // pairs
        return device * dc + k % local_sel * DILATION_MIN

    k, q = iota((n_dil, tiles), 0), iota((n_dil, tiles), 1)
    same_row = dil_row(k) == q // dc
    for p in range(DILATION_MIN):
        present = gathered_tissue(
            tissue, n_dil, lambda k: dil_row(k) + row_offset, lambda k: dil_col(k) + p, tiles
        )
        allowed = same_row & (present > 0.5)
        key_col = dil_col(k) + p
        apart = key_col ^ (column_offset + q % dc)
        for head in range(p, HEAD_COUNT, DILATION_MIN):
            stride = jnp.left_shift(jnp.int32(DILATION_MIN), dil_ref[head])
            segment = jnp.right_shift(jnp.int32(dc * n_col), seg_ref[head])
            phase_ok = ((key_col ^ head) & (stride - 1)) == 0
            ok = allowed & phase_ok & (apart < segment)
            bias_far[head, pl.ds(corners, n_dil)] = jnp.where(ok, 0.0, NEG_FILL)

    pl.when(has_down)(to_up.wait_recv)
    pl.when(has_up)(to_down.wait_recv)
    attend(mid_kv, 0, 2 * tiles, lambda head: bias_mid[pl.ds(0, 2 * tiles)], False)

    for t in pieces:
        for have, arrived, upward, downward in (
            (has_left, to_right[t], left_to_up[t], left_to_down[t]),
            (has_right, to_left[t], right_to_up[t], right_to_down[t]),
        ):
            pl.when(have)(arrived.wait_recv)
            pl.when(have & has_up & even)(upward.start)
            pl.when(have & has_down)(downward.start)
            pl.when(have & has_up & odd)(upward.start)

    for copy in key_spread:
        copy.wait_recv()
    key_swap.start()

    attend(
        mid_kv, 2 * tiles, tiles, lambda head: bias_mid[pl.ds(2 * tiles, tiles)], False
    )
    def corners_arrived(from_up, from_down):
        for t in pieces:
            pl.when(has_left & has_up & from_up)(left_to_down[t].wait_recv)
            pl.when(has_right & has_up & from_up)(right_to_down[t].wait_recv)
            pl.when(has_left & has_down & from_down)(left_to_up[t].wait_recv)
            pl.when(has_right & has_down & from_down)(right_to_up[t].wait_recv)

    def far_stage(begin, count):
        attend(far_kv, begin, count, lambda head: bias_far[head, pl.ds(begin, count)], False)

    corners_arrived(odd, even)
    far_stage(pl.multiple_of((1 - row % 2) * tiles, tiles), tiles)
    for copy in [key_swap] + value_spread + value_relay:
        copy.wait_recv()
    far_stage(corners, n_dil)
    corners_arrived(even, odd)

    @pl.when((has_up & even) | (has_down & odd))
    def _():
        far_stage(pl.multiple_of(row % 2 * tiles, tiles), tiles)

    finished = [numer[head] * (1.0 / total[head]) for head in range(HEAD_COUNT)]
    out_ref[...] = jnp.concatenate(finished, axis=0).T.astype(BF16)

    pl.when(has_up)(to_up.wait_send)
    pl.when(has_down)(to_down.wait_send)
    for t in pieces:
        pl.when(has_left)(to_left[t].wait_send)
        pl.when(has_right)(to_right[t].wait_send)
        pl.when(has_left & has_up)(left_to_up[t].wait_send)
        pl.when(has_left & has_down)(left_to_down[t].wait_send)
        pl.when(has_right & has_up)(right_to_up[t].wait_send)
        pl.when(has_right & has_down)(right_to_down[t].wait_send)
    for copy in key_spread + value_spread + value_relay + [value_swap, key_swap]:
        copy.wait_send()


def solution(mesh):
    n_row, n_col = mesh.shape["row"], mesh.shape["col"]

    def per_device(q, k, v, tissue, dilation_levels, segment_levels, output_matrix):
        dr, dc, width = q.shape
        tiles = dr * dc
        sel = tiles // DILATION_MIN
        groups = HEAD_COUNT // HEADS_TOGETHER
        hbm = pl.BlockSpec(memory_space=pltpu.HBM)
        vmem = pl.BlockSpec(memory_space=pltpu.VMEM)
        smem = pl.BlockSpec(memory_space=pltpu.SMEM)
        out = pl.pallas_call(
            functools.partial(kernel, n_row, n_col, dr, dc),
            out_shape=jax.ShapeDtypeStruct((tiles, width), BF16),
            in_specs=[hbm, hbm, hbm, vmem, smem, smem],
            out_specs=vmem,
            scratch_shapes=[
                pltpu.VMEM((tiles, width), BF16),
                pltpu.VMEM((groups, HEADS_TOGETHER * tiles, 256), BF16),
                pltpu.VMEM((2, tiles, width), BF16),
                pltpu.VMEM((2, 3 * tiles, width), BF16),
                pltpu.VMEM((2, 2 * tiles + sel * n_col, width), BF16),
                pltpu.VMEM((2, tiles, width), BF16),
                pltpu.VMEM((2, sel, width), BF16),
                pltpu.VMEM((tiles, tiles), F32),
                pltpu.VMEM((3 * tiles, tiles), F32),
                pltpu.VMEM((HEAD_COUNT, 2 * tiles + sel * n_col, tiles), F32),
                pltpu.VMEM((HEAD_COUNT, width // HEAD_COUNT, tiles), F32),
                pltpu.VMEM((HEAD_COUNT, 1, tiles), F32),
                pltpu.VMEM((HEAD_COUNT, 1, tiles), F32),
                pltpu.SemaphoreType.DMA((3,)),
                pltpu.SemaphoreType.DMA((26,)),
                pltpu.SemaphoreType.DMA((26,)),
                pltpu.SemaphoreType.DMA((2 * n_col,)),
                pltpu.SemaphoreType.DMA((2 * n_col,)),
            ],
            compiler_params=pltpu.CompilerParams(
                collective_id=0, has_side_effects=True, vmem_limit_bytes=56 * 1024 * 1024
            ),
        )(
            q.reshape(tiles, width), k.reshape(tiles, width), v.reshape(tiles, width),
            tissue, dilation_levels, segment_levels,
        )
        encoded = jnp.dot(out, output_matrix, preferred_element_type=F32).astype(BF16)
        return encoded.reshape(dr, dc, width)

    split = P("row", "col", None)
    return jax.shard_map(
        per_device,
        mesh=mesh,
        in_specs=(split, split, split, P(), P(), P(), P()),
        out_specs=split,
        check_vma=False,
    )
```
